512 devices in a mesh: depth: 16 (over x, y), tile: 32 (over z, core).
Axes of the slice: x: 4, y: 4, z: 16, core: 2. Of those that a mesh axis runs over, the one named last changes fastest.
Arguments:
- volume: bfloat16 [1024, 512, 1024], P('depth', 'tile'), may hold values from -6 to 6
Outputs:
- image: float32 [4, 512, 1024], P(None, 'tile', 'depth')
The draws below stay inside these ranges and needn't reach their ends.
All inputs are finite; a program needn't handle non-finite values.
Results may differ from the reference program's by a relative error of at most 0.0003.
Values may be sent and summed in bfloat16 or wider, within the bound.
A program may use at most 64 MiB of HBM per device.

```python
import jax
import jax.numpy as jnp
from jax import lax

CX = 16
NY = 1024
NZ = 1024
NX = 512
N_TILE = 32


def block_scale(rng, shape, split, low, largest):
    def one(position, parts):
        heights = jax.random.uniform(jax.random.fold_in(jax.random.fold_in(rng, 6), position), (parts,), jnp.float32, low / len(split), largest / len(split))
        return jnp.repeat(jnp.exp(heights), shape[position] // parts).reshape((-1,) + (1,) * (len(shape) - position - 1))

    level = one(*split[0])
    for cut in split[1:]:
        level = level * one(*cut)
    return level


def bell_draw(stream_key, shape, deviation, reach, cuts=(), held_as=jnp.bfloat16):
    array = deviation * jax.random.normal(stream_key, shape, jnp.float32)
    if cuts:
        array = array * block_scale(stream_key, shape, cuts, -0.22, 0.18)
    return jnp.clip(array, -reach, reach).astype(held_as)


def setup_inputs(seed: int = 0) -> dict:
    seeds = jax.random.split(jax.random.key(seed), 2)
    volume = bell_draw(seeds[0], (NZ, NX, NY), 1.0, 6.0, ((0, 16), (1, 32)))
    return {"volume": volume}


light_x = 1.0 / 3.0
light_y = 2.0 / 3.0
light_z = 2.0 / 3.0

def render(slab, step):
    core = slab[2:-2, 2:-2]
    grad_z = (slab[:-4, 2:-2] - 8.0 * slab[1:-3, 2:-2] + 8.0 * slab[3:-1, 2:-2] - slab[4:, 2:-2]) / 12.0
    grad_x = (slab[2:-2, :-4] - 8.0 * slab[2:-2, 1:-3] + 8.0 * slab[2:-2, 3:-1] - slab[2:-2, 4:]) / 12.0
    sided = jnp.pad(core, ((0, 0), (0, 0), (2, 2)))
    grad_y = (sided[:, :, :-4] - 8.0 * sided[:, :, 1:-3] + 8.0 * sided[:, :, 3:-1] - sided[:, :, 4:]) / 12.0
    facing = jnp.abs(light_x * grad_x + light_y * grad_y + light_z * grad_z)
    facing = facing * lax.rsqrt(grad_x * grad_x + grad_y * grad_y + grad_z * grad_z + 1.0)
    shading = 0.15 + 0.85 * facing
    optical = (1.0 + core * core) * step
    coverage = 1.0 - jnp.exp(-optical)
    running = jnp.cumsum(optical, axis=0)
    weight = jnp.exp(-(running - optical)) * coverage * shading
    red = lax.optimization_barrier(jnp.sum(weight * (1.0 + 0.5 * core), axis=0))
    green = lax.optimization_barrier(jnp.sum(weight * (1.0 - 0.3 * core + 0.2 * core * core), axis=0))
    blue = lax.optimization_barrier(jnp.sum(weight * (1.0 + 0.25 * core - 0.1 * core * core), axis=0))
    return (jnp.stack([red, green, blue], 0), jnp.exp(-running[-1]))

def reference(volume):
    padded = jnp.pad(volume, ((2, 2), (2, 2), (0, 0)))
    step = 1.0 / NZ

    def one_block(start):
        slab = lax.dynamic_slice(padded, (jnp.int32(0), start, jnp.int32(0)), (NZ + 4, CX + 4, NY)).astype(jnp.float32)
        color, transmit = render(slab, step)
        return jnp.concatenate([color, (1.0 - transmit)[None]], 0)
    starts = (jnp.arange(N_TILE) * CX).astype(jnp.int32)
    blocks = lax.map(one_block, starts)
    return jnp.transpose(blocks, (1, 0, 2, 3)).reshape(4, NX, NY)
```

```python
import functools
import math

import jax
import jax.numpy as jnp
from jax import lax
from jax.experimental import pallas as pl
from jax.experimental.pallas import tpu as pltpu
from jax.sharding import PartitionSpec as P

MESH = pl.DeviceIdType.MESH
LC = 256
OW = 64
ZB = 8
PAD = 128
BASE = 0.15 * 3.0 / 0.85
GAIN = 0.85 / 3.0


def taps(delta):
    value = jnp.where(delta == -2, 1.0, 0.0)
    value = jnp.where(delta == -1, -8.0, value)
    value = jnp.where(delta == 1, 8.0, value)
    return jnp.where(delta == 2, -1.0, value)


def stencil_zx():
    shape = (128, 256)
    out = lax.broadcasted_iota(jnp.int32, shape, 0)
    col = lax.broadcasted_iota(jnp.int32, shape, 1)
    zo, xo = out >> 4, out & 15
    zi, xi = (col >> 4) - 2, col & 15
    inside = col < 192
    gz = jnp.where(inside & (xi == xo), taps(zi - zo), 0.0)
    gx = jnp.where(inside & (zi == zo), taps(xi - xo), 0.0)
    k = col - 192
    right = k >= 16
    k = k & 15
    near = (col >= 192) & (col < 224) & ((k >> 1) == zo)
    pos = (k & 1) + jnp.where(right, 16, -2)
    gx = gx + jnp.where(near, taps(pos - xo), 0.0)
    return gx, gz, gx + 2.0 * gz


def kernel(nd, nt, v_ref, o_ref, vp, xhl, xhr, elo, ehi, gy2, gyq, wt, ss, dzx, dy, sb, rb,
           load_sem, zs, zr, xs, xr, cs, cr):
    nz, cx, ny = v_ref.shape
    nc = ny // LC
    per = LC // OW
    d = lax.axis_index("depth")
    t = lax.axis_index("tile")
    step = 1.0 / (nz * nd)
    scale = step * math.log2(math.e)

    barrier = pltpu.get_barrier_semaphore()
    for i in range(1, nd):
        pl.semaphore_signal(barrier, inc=1, device_id=(lax.rem(d + i, nd), t), device_id_type=MESH)

    @pl.when(t > 0)
    def _():
        pl.semaphore_signal(barrier, inc=1, device_id=(d, t - 1), device_id_type=MESH)

    @pl.when(t < nt - 1)
    def _():
        pl.semaphore_signal(barrier, inc=1, device_id=(d, t + 1), device_id_type=MESH)

    def chunk(k):
        return lax.rem(d // per + 1 + k, nc)

    def load(k):
        lane = pl.multiple_of(chunk(k) * LC, LC)
        return pltpu.make_async_copy(
            v_ref.at[:, :, pl.ds(lane, LC)],
            vp.at[pl.ds(2, nz), :, pl.ds(pl.multiple_of(lane + PAD, PAD), LC)],
            load_sem.at[k],
        )

    for k in range(nc):
        load(k).start()

    zeros = jnp.zeros((nz, cx, PAD), jnp.bfloat16)
    vp[2 : 2 + nz, :, 0:PAD] = zeros
    vp[2 : 2 + nz, :, PAD + ny :] = zeros

    @pl.when(d == 0)
    def _():
        vp[0:2] = jnp.zeros((2, cx, ny + 2 * PAD), jnp.bfloat16)

    @pl.when(d == nd - 1)
    def _():
        vp[nz + 2 :] = jnp.zeros((2, cx, ny + 2 * PAD), jnp.bfloat16)

    @pl.when(t == 0)
    def _():
        xhl[...] = jnp.zeros(xhl.shape, jnp.bfloat16)

    @pl.when(t == nt - 1)
    def _():
        xhr[...] = jnp.zeros(xhr.shape, jnp.bfloat16)

    gx, gz, both = stencil_zx()
    dzx[0:128] = gx.astype(jnp.bfloat16)
    dzx[128:256] = gz.astype(jnp.bfloat16)
    dzx[256:384] = both.astype(jnp.bfloat16)
    src = lax.broadcasted_iota(jnp.int32, (LC + 2 * PAD, LC), 0)
    dst = lax.broadcasted_iota(jnp.int32, (LC + 2 * PAD, LC), 1)
    dy[...] = (2.0 * taps(src - PAD - dst)).astype(jnp.bfloat16)

    def z_up():
        return pltpu.make_async_remote_copy(
            src_ref=v_ref.at[pl.ds(nz - 2, 2)],
            dst_ref=vp.at[pl.ds(0, 2), :, pl.ds(PAD, ny)],
            send_sem=zs.at[0], recv_sem=zr.at[0],
            device_id=(lax.rem(d + 1, nd), t), device_id_type=MESH,
        )

    def z_down():
        return pltpu.make_async_remote_copy(
            src_ref=v_ref.at[pl.ds(0, 2)],
            dst_ref=vp.at[pl.ds(nz + 2, 2), :, pl.ds(PAD, ny)],
            send_sem=zs.at[1], recv_sem=zr.at[1],
            device_id=(lax.rem(d + nd - 1, nd), t), device_id_type=MESH,
        )

    def x_up(k):
        lane = pl.ds(pl.multiple_of(chunk(k) * LC, LC), LC)
        return pltpu.make_async_remote_copy(
            src_ref=ehi.at[:, lane], dst_ref=xhl.at[:, lane],
            send_sem=xs.at[0, k], recv_sem=xr.at[0, k],
            device_id=(d, lax.rem(t + 1, nt)), device_id_type=MESH,
        )

    def x_down(k):
        lane = pl.ds(pl.multiple_of(chunk(k) * LC, LC), LC)
        return pltpu.make_async_remote_copy(
            src_ref=elo.at[:, lane], dst_ref=xhr.at[:, lane],
            send_sem=xs.at[1, k], recv_sem=xr.at[1, k],
            device_id=(d, lax.rem(t + nt - 1, nt)), device_id_type=MESH,
        )

    for k in range(nc):
        load(k).wait()
        lane = pl.multiple_of(chunk(k) * LC, LC)
        rows = vp[2 : 2 + nz, :, pl.ds(pl.multiple_of(lane + PAD, PAD), LC)]
        elo[:, pl.ds(lane, LC)] = rows[:, 0:2].reshape(nz * 2, LC)
        ehi[:, pl.ds(lane, LC)] = rows[:, cx - 2 : cx].reshape(nz * 2, LC)
        if k == 0:
            waits = nd - 1 + (t > 0).astype(jnp.int32) + (t < nt - 1).astype(jnp.int32)
            pl.semaphore_wait(barrier, waits)

            @pl.when(d < nd - 1)
            def _():
                z_up().start()

            @pl.when(d > 0)
            def _():
                z_down().start()

        @pl.when(t < nt - 1)
        def _():
            x_up(k).start()

        @pl.when(t > 0)
        def _():
            x_down(k).start()

    def before_halo(k, _):
        lane = pl.multiple_of(chunk(k) * LC, LC)
        total = jnp.zeros((cx, LC), jnp.float32)
        last = jnp.ones((cx, LC), jnp.float32)
        part = min(256 // cx, nz)
        for z0 in range(0, nz, part):
            slab = vp[2 + z0 : 2 + z0 + part, :, pl.ds(lane, LC + 2 * PAD)]
            slab = slab.reshape(part * cx, LC + 2 * PAD)
            g = jnp.dot(slab, dy[...], preferred_element_type=jnp.float32)
            gy2[k, z0 * cx : (z0 + part) * cx] = g
            gyq[k, z0 * cx : (z0 + part) * cx] = g * g * 0.25 + 144.0
            for z in range(z0, z0 + part):
                f = vp[2 + z, :, pl.ds(pl.multiple_of(lane + PAD, PAD), LC)].astype(jnp.float32)
                total = total + f * f
                now = jnp.exp2(total * -scale - scale * (z + 1))
                wt[k, z * cx : (z + 1) * cx] = last - now
                last = now
        ss[k] = total * scale + scale * nz
        return 0

    lax.fori_loop(0, nc, before_halo, 0)

    @pl.when(d > 0)
    def _():
        z_up().wait_recv()

    @pl.when(d < nd - 1)
    def _():
        z_down().wait_recv()

    low = lax.broadcasted_iota(jnp.int32, (cx, 128), 1) < OW

    def send(owner):
        return pltpu.make_async_remote_copy(
            src_ref=sb.at[owner], dst_ref=rb.at[d],
            send_sem=cs.at[owner], recv_sem=cr.at[d],
            device_id=(owner, t), device_id_type=MESH,
        )

    def after_halo(k, _):
        @pl.when(t > 0)
        def _():
            x_up(k).wait_recv()

        @pl.when(t < nt - 1)
        def _():
            x_down(k).wait_recv()

        lane = pl.multiple_of(chunk(k) * LC, LC)
        inner = pl.multiple_of(lane + PAD, PAD)
        m0 = jnp.zeros((cx, LC), jnp.float32)
        m1 = m0
        m2 = m0
        for z0 in range(0, nz, ZB):
            slab = jnp.concatenate(
                [
                    vp[z0 : z0 + ZB + 4, :, pl.ds(inner, LC)].reshape((ZB + 4) * cx, LC),
                    xhl[z0 * 2 : (z0 + ZB) * 2, pl.ds(lane, LC)],
                    xhr[z0 * 2 : (z0 + ZB) * 2, pl.ds(lane, LC)],
                    jnp.zeros((32, LC), jnp.bfloat16),
                ],
                axis=0,
            )
            g = jnp.dot(dzx[...], slab, preferred_element_type=jnp.float32)
            for j in range(ZB):
                here = slice((z0 + j) * cx, (z0 + j + 1) * cx)
                gx = g[j * cx : (j + 1) * cx]
                gz = g[128 + j * cx : 128 + (j + 1) * cx]
                facing = jnp.abs(g[256 + j * cx : 256 + (j + 1) * cx] + gy2[k, here])
                facing = facing * lax.rsqrt(gx * gx + gz * gz + gyq[k, here])
                w = wt[k, here] * (facing + BASE)
                f = vp[2 + z0 + j, :, pl.ds(inner, LC)].astype(jnp.float32)
                wf = w * f
                m0 = m0 + w
                m1 = m1 + wf
                m2 = m2 + wf * f
        s = ss[k]
        for q in range(per):
            owner = chunk(k) * per + q
            part = slice((q // 2) * 128, (q // 2 + 1) * 128)
            a, b, c, e = m0[:, part], m1[:, part], m2[:, part], s[:, part]
            if q % 2 == 0:
                first = jnp.where(low, a, pltpu.roll(b, OW, 1))
                second = jnp.where(low, c, pltpu.roll(e, OW, 1))
            else:
                first = jnp.where(low, pltpu.roll(a, OW, 1), b)
                second = jnp.where(low, pltpu.roll(c, OW, 1), e)
            sb[owner, 0] = first
            sb[owner, 1] = second

            @pl.when(owner != d)
            def _():
                send(owner).start()

        return 0

    lax.fori_loop(0, nc, after_halo, 0)
    rb[d] = sb[d]

    for i in range(nd):

        @pl.when(d != i)
        def _():
            pltpu.make_async_remote_copy(
                src_ref=sb.at[i], dst_ref=rb.at[i],
                send_sem=cs.at[i], recv_sem=cr.at[i],
                device_id=(d, t), device_id_type=MESH,
            ).wait_recv()

    ahead = jnp.zeros((cx, 128), jnp.float32)
    acc0 = ahead
    acc1 = ahead
    for i in range(nd):
        p0, p1 = rb[i, 0], rb[i, 1]
        through = jnp.exp2(-ahead)
        acc0 = acc0 + through * p0
        acc1 = acc1 + through * p1
        ahead = ahead + jnp.where(low, pltpu.roll(p1, OW, 1), p1)
    a = acc0 * GAIN
    b = pltpu.roll(a, OW, 1)
    c = acc1 * GAIN
    o_ref[0] = (a + 0.5 * b)[:, :OW]
    o_ref[1] = (a - 0.3 * b + 0.2 * c)[:, :OW]
    o_ref[2] = (a + 0.25 * b - 0.1 * c)[:, :OW]
    o_ref[3] = (1.0 - jnp.exp2(-ahead))[:, :OW]

    @pl.when(d < nd - 1)
    def _():
        z_up().wait_send()

    @pl.when(d > 0)
    def _():
        z_down().wait_send()

    for k in range(nc):

        @pl.when(t < nt - 1)
        def _():
            x_up(k).wait_send()

        @pl.when(t > 0)
        def _():
            x_down(k).wait_send()

    for i in range(nd):

        @pl.when(d != i)
        def _():
            send(i).wait_send()


def solution(mesh):
    nd, nt = mesh.shape["depth"], mesh.shape["tile"]

    def body(volume):
        nz, cx, ny = volume.shape
        nc = ny // LC
        big = (nc, nz * cx, LC)
        return pl.pallas_call(
            functools.partial(kernel, nd, nt),
            out_shape=jax.ShapeDtypeStruct((4, cx, OW), jnp.float32),
            in_specs=[pl.BlockSpec(memory_space=pl.ANY)],
            out_specs=pl.BlockSpec(memory_space=pltpu.VMEM),
            scratch_shapes=[
                pltpu.VMEM((nz + 4, cx, ny + 2 * PAD), jnp.bfloat16),
                pltpu.VMEM((nz * 2, ny), jnp.bfloat16),
                pltpu.VMEM((nz * 2, ny), jnp.bfloat16),
                pltpu.VMEM((nz * 2, ny), jnp.bfloat16),
                pltpu.VMEM((nz * 2, ny), jnp.bfloat16),
                pltpu.VMEM(big, jnp.float32),
                pltpu.VMEM(big, jnp.float32),
                pltpu.VMEM(big, jnp.float32),
                pltpu.VMEM((nc, cx, LC), jnp.float32),
                pltpu.VMEM((384, 256), jnp.bfloat16),
                pltpu.VMEM((LC + 2 * PAD, LC), jnp.bfloat16),
                pltpu.VMEM((nd, 2, cx, 128), jnp.float32),
                pltpu.VMEM((nd, 2, cx, 128), jnp.float32),
                pltpu.SemaphoreType.DMA((nc,)),
                pltpu.SemaphoreType.DMA((2,)),
                pltpu.SemaphoreType.DMA((2,)),
                pltpu.SemaphoreType.DMA((2, nc)),
                pltpu.SemaphoreType.DMA((2, nc)),
                pltpu.SemaphoreType.DMA((nd,)),
                pltpu.SemaphoreType.DMA((nd,)),
            ],
            compiler_params=pltpu.CompilerParams(
                collective_id=0, has_side_effects=True, vmem_limit_bytes=60 * 2**20
            ),
        )(volume)

    return jax.shard_map(
        body,
        mesh=mesh,
        in_specs=(P("depth", "tile", None),),
        out_specs=P(None, "tile", "depth"),
        check_vma=False,
    )
```

```python
import functools
import math

import jax
import jax.numpy as jnp
import ml_dtypes
import numpy as np
from jax import lax
from jax.experimental import pallas as pl
from jax.experimental.pallas import tpu as pltpu
from jax.sharding import PartitionSpec as P

MESH = pl.DeviceIdType.MESH
LC = 256
OW = 64
ZB = 8
PAD = 128
BASE = 0.15 * 3.0 / 0.85 / math.sqrt(5.0)
GAIN = 0.85 / 3.0 * math.sqrt(5.0)


def taps(delta):
    value = np.zeros(delta.shape, np.float32)
    for offset, weight in ((-2, 1.0), (-1, -8.0), (1, 8.0), (2, -1.0)):
        value[delta == offset] = weight
    return value


def stencil_zx():
    out, col = np.indices((128, 256))
    zo, xo = out // 16, out % 16
    zi, xi = col // 16 - 2, col % 16
    inside = col < 192
    gz = np.where(inside & (xi == xo), taps(zi - zo), 0.0)
    gx = np.where(inside & (zi == zo), taps(xi - xo), 0.0)
    k = (col - 192) % 16
    near = (col >= 192) & (col < 224) & (k // 2 == zo)
    pos = k % 2 + np.where(col >= 208, 16, -2)
    gx = gx + np.where(near, taps(pos - xo), 0.0)
    return np.concatenate([gx + 2.0 * gz, 2.0 * gx - gz], 0).astype(ml_dtypes.bfloat16)


def stencil_y():
    src, dst = np.indices((LC + 2 * PAD, LC))
    return (2.0 * taps(src - PAD - dst)).astype(ml_dtypes.bfloat16)


def kernel(nd, nt, v_ref, dzx_ref, dy_ref, o_ref, vp, xhl, xhr, elo, ehi, gy2, gyq, wt, ss, dzx, dy,
           ysb, yrb, xsb, xrb, load_sem, mat_sem, zs, zr, xs, xr, ys, yr, cs, cr):
    nz, cx, ny = v_ref.shape
    nc = ny // LC
    per = LC // OW
    d = lax.axis_index("depth")
    t = lax.axis_index("tile")
    row, col = d // per, lax.rem(d, per)
    scale = math.log2(math.e) / (nz * nd)

    def chunk(k):
        return lax.rem(row + 1 + k, nc)

    def load(k):
        lane = pl.multiple_of(chunk(k) * LC, LC)
        return pltpu.make_async_copy(
            v_ref.at[:, :, pl.ds(lane, LC)],
            vp.at[pl.ds(2, nz), :, pl.ds(pl.multiple_of(lane + PAD, PAD), LC)],
            load_sem.at[k],
        )

    for k in range(nc):
        load(k).start()
    mats = (
        pltpu.make_async_copy(dy_ref, dy, mat_sem.at[0]),
        pltpu.make_async_copy(dzx_ref, dzx, mat_sem.at[1]),
    )
    for copy in mats:
        copy.start()

    barrier = pltpu.get_barrier_semaphore()

    def greet(depth, tile):
        pl.semaphore_signal(barrier, inc=1, device_id=(depth, tile), device_id_type=MESH)

    @pl.when(t > 0)
    def _():
        greet(d, t - 1)

    @pl.when(t < nt - 1)
    def _():
        greet(d, t + 1)

    crosses_up = (col == per - 1) & (d < nd - 1)
    crosses_down = (col == 0) & (d > 0)

    @pl.when(crosses_up)
    def _():
        greet(d + 1, t)

    @pl.when(crosses_down)
    def _():
        greet(d - 1, t)

    for i in range(1, per):
        greet(row * per + lax.rem(col + i, per), t)
    for i in range(1, nc):
        greet(lax.rem(row + i, nc) * per + col, t)

    zeros = jnp.zeros((nz, cx, PAD), jnp.bfloat16)
    vp[2 : 2 + nz, :, 0:PAD] = zeros
    vp[2 : 2 + nz, :, PAD + ny :] = zeros

    @pl.when(d == 0)
    def _():
        vp[0:2] = jnp.zeros((2, cx, ny + 2 * PAD), jnp.bfloat16)

    @pl.when(d == nd - 1)
    def _():
        vp[nz + 2 :] = jnp.zeros((2, cx, ny + 2 * PAD), jnp.bfloat16)

    @pl.when(t == 0)
    def _():
        xhl[...] = jnp.zeros(xhl.shape, jnp.bfloat16)

    @pl.when(t == nt - 1)
    def _():
        xhr[...] = jnp.zeros(xhr.shape, jnp.bfloat16)

    def z_up():
        return pltpu.make_async_remote_copy(
            src_ref=v_ref.at[pl.ds(nz - 2, 2)],
            dst_ref=vp.at[pl.ds(0, 2), :, pl.ds(PAD, ny)],
            send_sem=zs.at[0], recv_sem=zr.at[0],
            device_id=(lax.rem(d + 1, nd), t), device_id_type=MESH,
        )

    def z_down():
        return pltpu.make_async_remote_copy(
            src_ref=v_ref.at[pl.ds(0, 2)],
            dst_ref=vp.at[pl.ds(nz + 2, 2), :, pl.ds(PAD, ny)],
            send_sem=zs.at[1], recv_sem=zr.at[1],
            device_id=(lax.rem(d + nd - 1, nd), t), device_id_type=MESH,
        )

    def x_up(k):
        lane = pl.ds(pl.multiple_of(chunk(k) * LC, LC), LC)
        return pltpu.make_async_remote_copy(
            src_ref=ehi.at[:, lane], dst_ref=xhl.at[:, lane],
            send_sem=xs.at[0, k], recv_sem=xr.at[0, k],
            device_id=(d, lax.rem(t + 1, nt)), device_id_type=MESH,
        )

    def x_down(k):
        lane = pl.ds(pl.multiple_of(chunk(k) * LC, LC), LC)
        return pltpu.make_async_remote_copy(
            src_ref=elo.at[:, lane], dst_ref=xhr.at[:, lane],
            send_sem=xs.at[1, k], recv_sem=xr.at[1, k],
            device_id=(d, lax.rem(t + nt - 1, nt)), device_id_type=MESH,
        )

    for k in range(nc):
        load(k).wait()
        lane = pl.multiple_of(chunk(k) * LC, LC)
        rows = vp[2 : 2 + nz, :, pl.ds(pl.multiple_of(lane + PAD, PAD), LC)]
        elo[:, pl.ds(lane, LC)] = rows[:, 0:2].reshape(nz * 2, LC)
        ehi[:, pl.ds(lane, LC)] = rows[:, cx - 2 : cx].reshape(nz * 2, LC)
        if k == 0:
            waits = per - 1 + nc - 1
            for there in (t > 0, t < nt - 1, crosses_up, crosses_down):
                waits = waits + there.astype(jnp.int32)
            pl.semaphore_wait(barrier, waits)

            @pl.when(d < nd - 1)
            def _():
                z_up().start()

            @pl.when(d > 0)
            def _():
                z_down().start()

        @pl.when(t < nt - 1)
        def _():
            x_up(k).start()

        @pl.when(t > 0)
        def _():
            x_down(k).start()

    for copy in mats:
        copy.wait()

    def before_halo(k, _):
        lane = pl.multiple_of(chunk(k) * LC, LC)
        total = jnp.zeros((cx, LC), jnp.float32)
        last = jnp.ones((cx, LC), jnp.float32)
        part = min(256 // cx, nz)
        for z0 in range(0, nz, part):
            slab = vp[2 + z0 : 2 + z0 + part, :, pl.ds(lane, LC + 2 * PAD)]
            slab = slab.reshape(part * cx, LC + 2 * PAD)
            g = jnp.dot(slab, dy[...], preferred_element_type=jnp.float32)
            gy2[k, z0 * cx : (z0 + part) * cx] = g
            gyq[k, z0 * cx : (z0 + part) * cx] = g * g * 1.25 + 720.0
            for z in range(z0, z0 + part):
                f = vp[2 + z, :, pl.ds(pl.multiple_of(lane + PAD, PAD), LC)].astype(jnp.float32)
                total = total + f * f
                now = jnp.exp2(total * -scale - scale * (z + 1))
                wt[k, z * cx : (z + 1) * cx] = last - now
                last = now
        ss[k] = total * scale + scale * nz
        return 0

    lax.fori_loop(0, nc, before_halo, 0)

    @pl.when(d > 0)
    def _():
        z_up().wait_recv()

    @pl.when(d < nd - 1)
    def _():
        z_down().wait_recv()

    low = lax.broadcasted_iota(jnp.int32, (cx, 128), 1) < OW

    def y_send(k, q):
        return pltpu.make_async_remote_copy(
            src_ref=ysb.at[k, q], dst_ref=yrb.at[k, col],
            send_sem=ys.at[k, q], recv_sem=yr.at[k, col],
            device_id=(row * per + q, t), device_id_type=MESH,
        )

    def y_arrival(k, q):
        return pltpu.make_async_remote_copy(
            src_ref=ysb.at[k, q], dst_ref=yrb.at[k, q],
            send_sem=ys.at[k, q], recv_sem=yr.at[k, q],
            device_id=(d, t), device_id_type=MESH,
        )

    def x_send(k):
        return pltpu.make_async_remote_copy(
            src_ref=xsb.at[k], dst_ref=xrb.at[row],
            send_sem=cs.at[k], recv_sem=cr.at[row],
            device_id=(chunk(k) * per + col, t), device_id_type=MESH,
        )

    def x_arrival(r):
        return pltpu.make_async_remote_copy(
            src_ref=xsb.at[0], dst_ref=xrb.at[r],
            send_sem=cs.at[0], recv_sem=cr.at[r],
            device_id=(d, t), device_id_type=MESH,
        )

    def composite(parts):
        ahead = jnp.zeros((cx, 128), jnp.float32)
        acc0 = ahead
        acc1 = ahead
        for p0, p1 in parts:
            through = jnp.exp2(-ahead)
            acc0 = acc0 + through * p0
            acc1 = acc1 + through * p1
            ahead = ahead + jnp.where(low, pltpu.roll(p1, OW, 1), p1)
        return acc0, acc1, ahead

    def join_row(k):
        for q in range(per):

            @pl.when(q != col)
            def _():
                y_arrival(k, q).wait_recv()

        return composite([(yrb[k, q, 0], yrb[k, q, 1]) for q in range(per)])

    def after_halo(k, _):
        @pl.when(t > 0)
        def _():
            x_up(k).wait_recv()

        @pl.when(t < nt - 1)
        def _():
            x_down(k).wait_recv()

        lane = pl.multiple_of(chunk(k) * LC, LC)
        inner = pl.multiple_of(lane + PAD, PAD)
        m0 = jnp.zeros((cx, LC), jnp.float32)
        m1 = m0
        m2 = m0
        for z0 in range(0, nz, ZB):
            slab = jnp.concatenate(
                [
                    vp[z0 : z0 + ZB + 4, :, pl.ds(inner, LC)].reshape((ZB + 4) * cx, LC),
                    xhl[z0 * 2 : (z0 + ZB) * 2, pl.ds(lane, LC)],
                    xhr[z0 * 2 : (z0 + ZB) * 2, pl.ds(lane, LC)],
                    jnp.zeros((32, LC), jnp.bfloat16),
                ],
                axis=0,
            )
            g = jnp.dot(dzx[...], slab, preferred_element_type=jnp.float32)
            for j in range(ZB):
                here = slice((z0 + j) * cx, (z0 + j + 1) * cx)
                p = g[j * cx : (j + 1) * cx]
                q = g[128 + j * cx : 128 + (j + 1) * cx]
                facing = jnp.abs(p + gy2[k, here])
                facing = facing * lax.rsqrt(p * p + q * q + gyq[k, here])
                w = wt[k, here] * (facing + BASE)
                f = vp[2 + z0 + j, :, pl.ds(inner, LC)].astype(jnp.float32)
                wf = w * f
                m0 = m0 + w
                m1 = m1 + wf
                m2 = m2 + wf * f
        s = ss[k]
        for q in range(per):
            part = slice((q // 2) * 128, (q // 2 + 1) * 128)
            a, b, c, e = m0[:, part], m1[:, part], m2[:, part], s[:, part]
            if q % 2 == 0:
                first = jnp.where(low, a, pltpu.roll(b, OW, 1))
                second = jnp.where(low, c, pltpu.roll(e, OW, 1))
            else:
                first = jnp.where(low, pltpu.roll(a, OW, 1), b)
                second = jnp.where(low, pltpu.roll(c, OW, 1), e)
            ysb[k, q, 0] = first
            ysb[k, q, 1] = second

            @pl.when(q != col)
            def _():
                y_send(k, q).start()

            @pl.when(q == col)
            def _():
                yrb[k, q, 0] = first
                yrb[k, q, 1] = second

        @pl.when(k > 0)
        def _():
            acc0, acc1, ahead = join_row(k - 1)
            xsb[k - 1, 0] = acc0
            xsb[k - 1, 1] = jnp.where(low, acc1, ahead)
            x_send(k - 1).start()

        return 0

    lax.fori_loop(0, nc, after_halo, 0)
    acc0, acc1, ahead = join_row(nc - 1)
    xrb[row, 0] = acc0
    xrb[row, 1] = jnp.where(low, acc1, ahead)
    for r in range(nc):

        @pl.when(r != row)
        def _():
            x_arrival(r).wait_recv()

    acc0, acc1, ahead = composite([(xrb[r, 0], xrb[r, 1]) for r in range(nc)])
    a = acc0 * GAIN
    b = pltpu.roll(a, OW, 1)
    c = acc1 * GAIN
    o_ref[0] = (a + 0.5 * b)[:, :OW]
    o_ref[1] = (a - 0.3 * b + 0.2 * c)[:, :OW]
    o_ref[2] = (a + 0.25 * b - 0.1 * c)[:, :OW]
    o_ref[3] = (1.0 - jnp.exp2(-ahead))[:, :OW]

    @pl.when(d < nd - 1)
    def _():
        z_up().wait_send()

    @pl.when(d > 0)
    def _():
        z_down().wait_send()

    for k in range(nc):

        @pl.when(t < nt - 1)
        def _():
            x_up(k).wait_send()

        @pl.when(t > 0)
        def _():
            x_down(k).wait_send()

        for q in range(per):

            @pl.when(q != col)
            def _():
                y_send(k, q).wait_send()

        if k < nc - 1:
            x_send(k).wait_send()


def solution(mesh):
    nd, nt = mesh.shape["depth"], mesh.shape["tile"]

    def body(volume):
        nz, cx, ny = volume.shape
        nc, per = ny // LC, LC // OW
        big = (nc, nz * cx, LC)
        return pl.pallas_call(
            functools.partial(kernel, nd, nt),
            out_shape=jax.ShapeDtypeStruct((4, cx, OW), jnp.float32),
            in_specs=[pl.BlockSpec(memory_space=pl.ANY)] * 3,
            out_specs=pl.BlockSpec(memory_space=pltpu.VMEM),
            scratch_shapes=[
                pltpu.VMEM((nz + 4, cx, ny + 2 * PAD), jnp.bfloat16),
                pltpu.VMEM((nz * 2, ny), jnp.bfloat16),
                pltpu.VMEM((nz * 2, ny), jnp.bfloat16),
                pltpu.VMEM((nz * 2, ny), jnp.bfloat16),
                pltpu.VMEM((nz * 2, ny), jnp.bfloat16),
                pltpu.VMEM(big, jnp.float32),
                pltpu.VMEM(big, jnp.float32),
                pltpu.VMEM(big, jnp.float32),
                pltpu.VMEM((nc, cx, LC), jnp.float32),
                pltpu.VMEM((256, 256), jnp.bfloat16),
                pltpu.VMEM((LC + 2 * PAD, LC), jnp.bfloat16),
                pltpu.VMEM((nc, per, 2, cx, 128), jnp.float32),
                pltpu.VMEM((nc, per, 2, cx, 128), jnp.float32),
                pltpu.VMEM((nc, 2, cx, 128), jnp.float32),
                pltpu.VMEM((nc, 2, cx, 128), jnp.float32),
                pltpu.SemaphoreType.DMA((nc,)),
                pltpu.SemaphoreType.DMA((2,)),
                pltpu.SemaphoreType.DMA((2,)),
                pltpu.SemaphoreType.DMA((2,)),
                pltpu.SemaphoreType.DMA((2, nc)),
                pltpu.SemaphoreType.DMA((2, nc)),
                pltpu.SemaphoreType.DMA((nc, per)),
                pltpu.SemaphoreType.DMA((nc, per)),
                pltpu.SemaphoreType.DMA((nc,)),
                pltpu.SemaphoreType.DMA((nc,)),
            ],
            compiler_params=pltpu.CompilerParams(
                collective_id=0, has_side_effects=True, vmem_limit_bytes=60 * 2**20
            ),
        )(volume, jnp.asarray(stencil_zx()), jnp.asarray(stencil_y()))

    return jax.shard_map(
        body,
        mesh=mesh,
        in_specs=(P("depth", "tile", None),),
        out_specs=P(None, "tile", "depth"),
        check_vma=False,
    )
```

```python
import functools
import math

import jax
import jax.numpy as jnp
import ml_dtypes
import numpy as np
from jax import lax
from jax.experimental import pallas as pl
from jax.experimental.pallas import tpu as pltpu
from jax.sharding import PartitionSpec as P

MESH = pl.DeviceIdType.MESH
LC = 256
OW = 64
ZB = 8
PAD = 128
BASE = 0.15 * 3.0 / 0.85 / math.sqrt(5.0)
CODE = 44.0
GAIN = 0.85 / 3.0 * math.sqrt(5.0)


def taps(delta):
    value = np.zeros(delta.shape, np.float32)
    for offset, weight in ((-2, 1.0), (-1, -8.0), (1, 8.0), (2, -1.0)):
        value[delta == offset] = weight
    return value


def stencil_zx():
    out, col = np.indices((128, 256))
    zo, xo = out // 16, out % 16
    zi, xi = col // 16 - 2, col % 16
    inside = col < 192
    gz = np.where(inside & (xi == xo), taps(zi - zo), 0.0)
    gx = np.where(inside & (zi == zo), taps(xi - xo), 0.0)
    k = (col - 192) % 16
    near = (col >= 192) & (col < 224) & (k // 2 == zo)
    pos = k % 2 + np.where(col >= 208, 16, -2)
    gx = gx + np.where(near, taps(pos - xo), 0.0)
    return np.concatenate([gx + 2.0 * gz, 2.0 * gx - gz], 0).astype(ml_dtypes.bfloat16)


def stencil_y():
    src, dst = np.indices((LC + 2 * PAD, LC))
    return (2.0 * taps(src - PAD - dst)).astype(ml_dtypes.bfloat16)


def encode(value):
    v = value * CODE
    v2 = v * v
    v4 = v2 * v2
    return (v4 * v4 * v2 * v).astype(jnp.bfloat16)


def decode(code):
    u = code.astype(jnp.float32)
    size = jnp.exp2(jnp.log2(jnp.maximum(jnp.abs(u), 1e-37)) * (1.0 / 11.0) - math.log2(CODE))
    return jnp.where(u < 0.0, -size, size)


def kernel(nd, nt, v_ref, dzx_ref, dy_ref, o_ref, vp, xhl, xhr, elo, ehi, gy2, gyq, wt, ss, dzx, dy,
           sb, rb, got, load_sem, mat_sem, zs, zr, xs, xr, cs, cr):
    nz, cx, ny = v_ref.shape
    nc = ny // LC
    per = LC // OW
    d = lax.axis_index("depth")
    t = lax.axis_index("tile")
    row, col = d // per, lax.rem(d, per)
    scale = math.log2(math.e) / (nz * nd)

    def chunk(k):
        if nc != 4:
            return lax.rem(row + 1 + k, nc)
        if isinstance(k, int):
            return lax.rem(row + (2, 1, 3, 0)[k], nc)
        return lax.rem(row + jnp.where(k == 3, 0, jnp.where(k == 2, 3, 2 - k)), nc)

    def load(k):
        lane = pl.multiple_of(chunk(k) * LC, LC)
        return pltpu.make_async_copy(
            v_ref.at[:, :, pl.ds(lane, LC)],
            vp.at[pl.ds(2, nz), :, pl.ds(pl.multiple_of(lane + PAD, PAD), LC)],
            load_sem.at[k],
        )

    for k in range(nc):
        load(k).start()
    mats = (
        pltpu.make_async_copy(dy_ref, dy, mat_sem.at[0]),
        pltpu.make_async_copy(dzx_ref, dzx, mat_sem.at[1]),
    )
    for copy in mats:
        copy.start()

    barrier = pltpu.get_barrier_semaphore()

    def greet(depth, tile):
        pl.semaphore_signal(barrier, inc=1, device_id=(depth, tile), device_id_type=MESH)

    @pl.when(t > 0)
    def _():
        greet(d, t - 1)

    @pl.when(t < nt - 1)
    def _():
        greet(d, t + 1)

    for i in (1, nd - 1, *range(2, nd - 1)):
        greet(lax.rem(d + i, nd), t)

    zeros = jnp.zeros((nz, cx, PAD), jnp.bfloat16)
    vp[2 : 2 + nz, :, 0:PAD] = zeros
    vp[2 : 2 + nz, :, PAD + ny :] = zeros

    @pl.when(d == 0)
    def _():
        vp[0:2] = jnp.zeros((2, cx, ny + 2 * PAD), jnp.bfloat16)

    @pl.when(d == nd - 1)
    def _():
        vp[nz + 2 :] = jnp.zeros((2, cx, ny + 2 * PAD), jnp.bfloat16)

    @pl.when(t == 0)
    def _():
        xhl[...] = jnp.zeros(xhl.shape, jnp.bfloat16)

    @pl.when(t == nt - 1)
    def _():
        xhr[...] = jnp.zeros(xhr.shape, jnp.bfloat16)

    def z_up():
        return pltpu.make_async_remote_copy(
            src_ref=v_ref.at[pl.ds(nz - 2, 2)],
            dst_ref=vp.at[pl.ds(0, 2), :, pl.ds(PAD, ny)],
            send_sem=zs.at[0], recv_sem=zr.at[0],
            device_id=(lax.rem(d + 1, nd), t), device_id_type=MESH,
        )

    def z_down():
        return pltpu.make_async_remote_copy(
            src_ref=v_ref.at[pl.ds(0, 2)],
            dst_ref=vp.at[pl.ds(nz + 2, 2), :, pl.ds(PAD, ny)],
            send_sem=zs.at[1], recv_sem=zr.at[1],
            device_id=(lax.rem(d + nd - 1, nd), t), device_id_type=MESH,
        )

    def x_up(k):
        lane = pl.ds(pl.multiple_of(chunk(k) * LC, LC), LC)
        return pltpu.make_async_remote_copy(
            src_ref=ehi.at[:, lane], dst_ref=xhl.at[:, lane],
            send_sem=xs.at[0, k], recv_sem=xr.at[0, k],
            device_id=(d, lax.rem(t + 1, nt)), device_id_type=MESH,
        )

    def x_down(k):
        lane = pl.ds(pl.multiple_of(chunk(k) * LC, LC), LC)
        return pltpu.make_async_remote_copy(
            src_ref=elo.at[:, lane], dst_ref=xhr.at[:, lane],
            send_sem=xs.at[1, k], recv_sem=xr.at[1, k],
            device_id=(d, lax.rem(t + nt - 1, nt)), device_id_type=MESH,
        )

    for k in range(nc):
        load(k).wait()
        lane = pl.multiple_of(chunk(k) * LC, LC)
        rows = vp[2 : 2 + nz, :, pl.ds(pl.multiple_of(lane + PAD, PAD), LC)]
        elo[:, pl.ds(lane, LC)] = rows[:, 0:2].reshape(nz * 2, LC)
        ehi[:, pl.ds(lane, LC)] = rows[:, cx - 2 : cx].reshape(nz * 2, LC)
        if k == 0:
            waits = nd - 1 + (t > 0).astype(jnp.int32) + (t < nt - 1).astype(jnp.int32)
            pl.semaphore_wait(barrier, waits)

            @pl.when(d < nd - 1)
            def _():
                z_up().start()

            @pl.when(d > 0)
            def _():
                z_down().start()

        @pl.when(t < nt - 1)
        def _():
            x_up(k).start()

        @pl.when(t > 0)
        def _():
            x_down(k).start()

    for copy in mats:
        copy.wait()

    def before_halo(k, _):
        lane = pl.multiple_of(chunk(k) * LC, LC)
        total = jnp.zeros((cx, LC), jnp.float32)
        last = jnp.ones((cx, LC), jnp.float32)
        part = min(256 // cx, nz)
        for z0 in range(0, nz, part):
            slab = vp[2 + z0 : 2 + z0 + part, :, pl.ds(lane, LC + 2 * PAD)]
            slab = slab.reshape(part * cx, LC + 2 * PAD)
            g = jnp.dot(slab, dy[...], preferred_element_type=jnp.float32)
            gy2[k, z0 * cx : (z0 + part) * cx] = g
            gyq[k, z0 * cx : (z0 + part) * cx] = g * g * 1.25 + 720.0
            for z in range(z0, z0 + part):
                f = vp[2 + z, :, pl.ds(pl.multiple_of(lane + PAD, PAD), LC)].astype(jnp.float32)
                total = total + f * f
                now = jnp.exp2(total * -scale - scale * (z + 1))
                wt[k, z * cx : (z + 1) * cx] = last - now
                last = now
        ss[k] = total * scale + scale * nz
        return 0

    lax.fori_loop(0, nc, before_halo, 0)

    @pl.when(d > 0)
    def _():
        z_up().wait_recv()

    @pl.when(d < nd - 1)
    def _():
        z_down().wait_recv()

    low = lax.broadcasted_iota(jnp.int32, (cx, 128), 1) < OW

    def send(owner):
        return pltpu.make_async_remote_copy(
            src_ref=sb.at[owner], dst_ref=rb.at[d],
            send_sem=cs.at[owner], recv_sem=cr.at[d],
            device_id=(owner, t), device_id_type=MESH,
        )

    def arrival(i):
        return pltpu.make_async_remote_copy(
            src_ref=sb.at[i], dst_ref=rb.at[i],
            send_sem=cs.at[i], recv_sem=cr.at[i],
            device_id=(d, t), device_id_type=MESH,
        )

    def after_halo(k, _):
        @pl.when(t > 0)
        def _():
            x_up(k).wait_recv()

        @pl.when(t < nt - 1)
        def _():
            x_down(k).wait_recv()

        lane = pl.multiple_of(chunk(k) * LC, LC)
        inner = pl.multiple_of(lane + PAD, PAD)
        m0 = jnp.zeros((cx, LC), jnp.float32)
        m1 = m0
        m2 = m0
        for z0 in range(0, nz, ZB):
            slab = jnp.concatenate(
                [
                    vp[z0 : z0 + ZB + 4, :, pl.ds(inner, LC)].reshape((ZB + 4) * cx, LC),
                    xhl[z0 * 2 : (z0 + ZB) * 2, pl.ds(lane, LC)],
                    xhr[z0 * 2 : (z0 + ZB) * 2, pl.ds(lane, LC)],
                    jnp.zeros((32, LC), jnp.bfloat16),
                ],
                axis=0,
            )
            g = jnp.dot(dzx[...], slab, preferred_element_type=jnp.float32)
            for j in range(ZB):
                here = slice((z0 + j) * cx, (z0 + j + 1) * cx)
                p = g[j * cx : (j + 1) * cx]
                q = g[128 + j * cx : 128 + (j + 1) * cx]
                facing = jnp.abs(p + gy2[k, here])
                facing = facing * lax.rsqrt(p * p + q * q + gyq[k, here])
                w = wt[k, here] * (facing + BASE)
                f = vp[2 + z0 + j, :, pl.ds(inner, LC)].astype(jnp.float32)
                wf = w * f
                m0 = m0 + w
                m1 = m1 + wf
                m2 = m2 + wf * f
        s = ss[k]
        for q in range(per):
            part = slice((q // 2) * 128, (q // 2 + 1) * 128)
            a, b, c, e = m0[:, part], m1[:, part], m2[:, part], s[:, part]
            if q % 2 == 0:
                first = jnp.where(low, a, pltpu.roll(b, OW, 1))
                second = jnp.where(low, c, pltpu.roll(e, OW, 1))
            else:
                first = jnp.where(low, pltpu.roll(a, OW, 1), b)
                second = jnp.where(low, pltpu.roll(c, OW, 1), e)
            owner = chunk(k) * per + q

            @pl.when(owner != d)
            def _():
                sb[owner, 0] = encode(first)
                sb[owner, 1] = encode(second)
                send(owner).start()

            @pl.when(owner == d)
            def _():
                got[d, 0] = first
                got[d, 1] = second

        return 0

    lax.fori_loop(0, nc, after_halo, 0)

    def take(r, q):
        @pl.when((r != row) | (q != col))
        def _():
            i = r * per + q
            arrival(i).wait_recv()
            got[i] = decode(rb[i])

    def other_row(n, _):
        for q in range(per):
            take(lax.rem(row + n, nc), q)
        return 0

    lax.fori_loop(1, nc + 1, other_row, 0)
    ahead = jnp.zeros((cx, 128), jnp.float32)
    acc0 = ahead
    acc1 = ahead
    for i in range(nd):
        p0, p1 = got[i, 0], got[i, 1]
        through = jnp.exp2(-ahead)
        acc0 = acc0 + through * p0
        acc1 = acc1 + through * p1
        ahead = ahead + jnp.where(low, pltpu.roll(p1, OW, 1), p1)
    a = acc0 * GAIN
    b = pltpu.roll(a, OW, 1)
    c = acc1 * GAIN
    o_ref[0] = (a + 0.5 * b)[:, :OW]
    o_ref[1] = (a - 0.3 * b + 0.2 * c)[:, :OW]
    o_ref[2] = (a + 0.25 * b - 0.1 * c)[:, :OW]
    o_ref[3] = (1.0 - jnp.exp2(-ahead))[:, :OW]

    @pl.when(d < nd - 1)
    def _():
        z_up().wait_send()

    @pl.when(d > 0)
    def _():
        z_down().wait_send()

    for k in range(nc):

        @pl.when(t < nt - 1)
        def _():
            x_up(k).wait_send()

        @pl.when(t > 0)
        def _():
            x_down(k).wait_send()

    for i in range(nd):

        @pl.when(d != i)
        def _():
            send(i).wait_send()


def solution(mesh):
    nd, nt = mesh.shape["depth"], mesh.shape["tile"]

    def body(volume):
        nz, cx, ny = volume.shape
        nc = ny // LC
        big = (nc, nz * cx, LC)
        return pl.pallas_call(
            functools.partial(kernel, nd, nt),
            out_shape=jax.ShapeDtypeStruct((4, cx, OW), jnp.float32),
            in_specs=[pl.BlockSpec(memory_space=pl.ANY)] * 3,
            out_specs=pl.BlockSpec(memory_space=pltpu.VMEM),
            scratch_shapes=[
                pltpu.VMEM((nz + 4, cx, ny + 2 * PAD), jnp.bfloat16),
                pltpu.VMEM((nz * 2, ny), jnp.bfloat16),
                pltpu.VMEM((nz * 2, ny), jnp.bfloat16),
                pltpu.VMEM((nz * 2, ny), jnp.bfloat16),
                pltpu.VMEM((nz * 2, ny), jnp.bfloat16),
                pltpu.VMEM(big, jnp.float32),
                pltpu.VMEM(big, jnp.float32),
                pltpu.VMEM(big, jnp.float32),
                pltpu.VMEM((nc, cx, LC), jnp.float32),
                pltpu.VMEM((256, 256), jnp.bfloat16),
                pltpu.VMEM((LC + 2 * PAD, LC), jnp.bfloat16),
                pltpu.VMEM((nd, 2, cx, 128), jnp.bfloat16),
                pltpu.VMEM((nd, 2, cx, 128), jnp.bfloat16),
                pltpu.VMEM((nd, 2, cx, 128), jnp.float32),
                pltpu.SemaphoreType.DMA((nc,)),
                pltpu.SemaphoreType.DMA((2,)),
                pltpu.SemaphoreType.DMA((2,)),
                pltpu.SemaphoreType.DMA((2,)),
                pltpu.SemaphoreType.DMA((2, nc)),
                pltpu.SemaphoreType.DMA((2, nc)),
                pltpu.SemaphoreType.DMA((nd,)),
                pltpu.SemaphoreType.DMA((nd,)),
            ],
            compiler_params=pltpu.CompilerParams(
                collective_id=0, has_side_effects=True, vmem_limit_bytes=60 * 2**20
            ),
        )(volume, jnp.asarray(stencil_zx()), jnp.asarray(stencil_y()))

    return jax.shard_map(
        body,
        mesh=mesh,
        in_specs=(P("depth", "tile", None),),
        out_specs=P(None, "tile", "depth"),
        check_vma=False,
    )
```

```python
import functools
import math

import jax
import jax.numpy as jnp
from jax import lax
from jax.experimental import pallas as pl
from jax.experimental.pallas import tpu as pltpu
from jax.sharding import PartitionSpec as P

MESH = pl.DeviceIdType.MESH
LC = 256
OW = 64
ZB = 8
PAD = 128
BASE = 0.15 * 3.0 / 0.85 / math.sqrt(5.0)
CODE = 44.0
GAIN = 0.85 / 3.0 * math.sqrt(5.0)


def taps(delta):
    value = jnp.where(delta == -2, 1.0, 0.0)
    value = jnp.where(delta == -1, -8.0, value)
    value = jnp.where(delta == 1, 8.0, value)
    return jnp.where(delta == 2, -1.0, value)


def stencil_zx():
    out = lax.broadcasted_iota(jnp.int32, (128, 256), 0)
    col = lax.broadcasted_iota(jnp.int32, (128, 256), 1)
    zo, xo = out >> 4, out & 15
    zi, xi = (col >> 4) - 2, col & 15
    inside = col < 192
    gz = jnp.where(inside & (xi == xo), taps(zi - zo), 0.0)
    k = col & 15
    pos = (k & 1) + jnp.where(col >= 208, 16, -2)
    plane = jnp.where(inside, zi, jnp.where(col < 224, k >> 1, -9))
    gx = jnp.where(plane == zo, taps(jnp.where(inside, xi, pos) - xo), 0.0)
    return gx + 2.0 * gz, 2.0 * gx - gz


def encode(value):
    v = value * CODE
    v2 = v * v
    v4 = v2 * v2
    return (v4 * v4 * v2 * v).astype(jnp.bfloat16)


def decode(code):
    u = code.astype(jnp.float32)
    size = jnp.exp2(jnp.log2(jnp.maximum(jnp.abs(u), 1e-37)) * (1.0 / 11.0) - math.log2(CODE))
    return jnp.where(u < 0.0, -size, size)


def kernel(nd, nt, v_ref, o_ref, vp, xhl, xhr, elo, ehi, gy2, gyq, wt, ss, dzx, dy,
           sb, rb, got, gbuf, load_sem, zs, zr, xs, xr, cs, cr):
    nz, cx, ny = v_ref.shape
    nc = ny // LC
    per = LC // OW
    d = lax.axis_index("depth")
    t = lax.axis_index("tile")
    row, col = d // per, lax.rem(d, per)
    scale = math.log2(math.e) / (nz * nd)

    def chunk(k, r=None):
        r = row if r is None else r
        if nc != 4:
            return lax.rem(r + 1 + k, nc)
        if isinstance(k, int):
            return lax.rem(r + (2, 1, 3, 0)[k], nc)
        return lax.rem(r + jnp.where(k == 3, 0, jnp.where(k == 2, 3, 2 - k)), nc)

    def load(k):
        lane = pl.multiple_of(chunk(k) * LC, LC)
        return pltpu.make_async_copy(
            v_ref.at[:, :, pl.ds(lane, LC)],
            vp.at[pl.ds(2, nz), :, pl.ds(pl.multiple_of(lane + PAD, PAD), LC)],
            load_sem.at[k],
        )

    for k in range(nc):
        load(k).start()

    barrier = pltpu.get_barrier_semaphore()

    def greet(depth, tile):
        pl.semaphore_signal(barrier, inc=1, device_id=(depth, tile), device_id_type=MESH)

    @pl.when(t > 0)
    def _():
        greet(d, t - 1)

    @pl.when(t < nt - 1)
    def _():
        greet(d, t + 1)

    for i in (1, nd - 1, *range(2, nd - 1)):
        greet(lax.rem(d + i, nd), t)

    zeros = jnp.zeros((nz, cx, PAD), jnp.bfloat16)
    vp[2 : 2 + nz, :, 0:PAD] = zeros
    vp[2 : 2 + nz, :, PAD + ny :] = zeros

    @pl.when(d == 0)
    def _():
        vp[0:2] = jnp.zeros((2, cx, ny + 2 * PAD), jnp.bfloat16)

    @pl.when(d == nd - 1)
    def _():
        vp[nz + 2 :] = jnp.zeros((2, cx, ny + 2 * PAD), jnp.bfloat16)

    @pl.when(t == 0)
    def _():
        xhl[...] = jnp.zeros(xhl.shape, jnp.bfloat16)

    @pl.when(t == nt - 1)
    def _():
        xhr[...] = jnp.zeros(xhr.shape, jnp.bfloat16)

    p_taps, q_taps = stencil_zx()
    dzx[0:128] = p_taps.astype(jnp.bfloat16)
    dzx[128:256] = q_taps.astype(jnp.bfloat16)
    src = lax.broadcasted_iota(jnp.int32, (PAD, LC), 0)
    dst = lax.broadcasted_iota(jnp.int32, (PAD, LC), 1)
    for i in range(0, LC + 2 * PAD, PAD):
        dy[i : i + PAD] = (2.0 * taps(src - dst + (i - PAD))).astype(jnp.bfloat16)

    def z_copy(k, up):
        there = lax.rem(d + (1 if up else nd - 1), nd)
        lane = pl.multiple_of(chunk(k, there // per) * LC, LC)
        return pltpu.make_async_remote_copy(
            src_ref=v_ref.at[pl.ds(nz - 2 if up else 0, 2), :, pl.ds(lane, LC)],
            dst_ref=vp.at[pl.ds(0 if up else nz + 2, 2), :, pl.ds(pl.multiple_of(lane + PAD, PAD), LC)],
            send_sem=zs.at[1 - up, k], recv_sem=zr.at[1 - up, k],
            device_id=(there, t), device_id_type=MESH,
        )

    def z_arrival(k, up):
        lane = pl.multiple_of(chunk(k) * LC, LC)
        return pltpu.make_async_remote_copy(
            src_ref=v_ref.at[pl.ds(0, 2), :, pl.ds(lane, LC)],
            dst_ref=vp.at[pl.ds(0 if up else nz + 2, 2), :, pl.ds(pl.multiple_of(lane + PAD, PAD), LC)],
            send_sem=zs.at[1 - up, k], recv_sem=zr.at[1 - up, k],
            device_id=(d, t), device_id_type=MESH,
        )

    def x_up(k):
        lane = pl.ds(pl.multiple_of(chunk(k) * LC, LC), LC)
        return pltpu.make_async_remote_copy(
            src_ref=ehi.at[:, lane], dst_ref=xhl.at[:, lane],
            send_sem=xs.at[0, k], recv_sem=xr.at[0, k],
            device_id=(d, lax.rem(t + 1, nt)), device_id_type=MESH,
        )

    def x_down(k):
        lane = pl.ds(pl.multiple_of(chunk(k) * LC, LC), LC)
        return pltpu.make_async_remote_copy(
            src_ref=elo.at[:, lane], dst_ref=xhr.at[:, lane],
            send_sem=xs.at[1, k], recv_sem=xr.at[1, k],
            device_id=(d, lax.rem(t + nt - 1, nt)), device_id_type=MESH,
        )

    for k in range(nc):
        load(k).wait()
        lane = pl.multiple_of(chunk(k) * LC, LC)
        rows = vp[2 : 2 + nz, :, pl.ds(pl.multiple_of(lane + PAD, PAD), LC)]
        elo[:, pl.ds(lane, LC)] = rows[:, 0:2].reshape(nz * 2, LC)
        ehi[:, pl.ds(lane, LC)] = rows[:, cx - 2 : cx].reshape(nz * 2, LC)
        if k == 0:
            waits = nd - 1 + (t > 0).astype(jnp.int32) + (t < nt - 1).astype(jnp.int32)
            pl.semaphore_wait(barrier, waits)

        @pl.when(t < nt - 1)
        def _():
            x_up(k).start()

        @pl.when(t > 0)
        def _():
            x_down(k).start()

        @pl.when(d < nd - 1)
        def _():
            z_copy(k, True).start()

        @pl.when(d > 0)
        def _():
            z_copy(k, False).start()

    def before_halo(k, _):
        lane = pl.multiple_of(chunk(k) * LC, LC)
        total = jnp.zeros((cx, LC), jnp.float32)
        last = jnp.ones((cx, LC), jnp.float32)
        part = min(256 // cx, nz)
        for z0 in range(0, nz, part):
            slab = vp[2 + z0 : 2 + z0 + part, :, pl.ds(lane, LC + 2 * PAD)]
            slab = slab.reshape(part * cx, LC + 2 * PAD)
            g = jnp.dot(slab, dy[...], preferred_element_type=jnp.float32)
            gy2[k, z0 * cx : (z0 + part) * cx] = g
            gyq[k, z0 * cx : (z0 + part) * cx] = g * g * 1.25 + 720.0
            for z in range(z0, z0 + part):
                f = vp[2 + z, :, pl.ds(pl.multiple_of(lane + PAD, PAD), LC)].astype(jnp.float32)
                total = total + f * f
                now = jnp.exp2(total * -scale - scale * (z + 1))
                wt[k, z * cx : (z + 1) * cx] = last - now
                last = now
        ss[k] = total * scale + scale * nz
        return 0

    lax.fori_loop(0, nc, before_halo, 0)

    low = lax.broadcasted_iota(jnp.int32, (cx, 128), 1) < OW

    def send(owner):
        return pltpu.make_async_remote_copy(
            src_ref=sb.at[owner], dst_ref=rb.at[d],
            send_sem=cs.at[owner], recv_sem=cr.at[d],
            device_id=(owner, t), device_id_type=MESH,
        )

    def arrival(i):
        return pltpu.make_async_remote_copy(
            src_ref=sb.at[i], dst_ref=rb.at[i],
            send_sem=cs.at[i], recv_sem=cr.at[i],
            device_id=(d, t), device_id_type=MESH,
        )

    def wait_halo(k):
        @pl.when(t > 0)
        def _():
            x_up(k).wait_recv()

        @pl.when(t < nt - 1)
        def _():
            x_down(k).wait_recv()

        @pl.when(d > 0)
        def _():
            z_arrival(k, True).wait_recv()

        @pl.when(d < nd - 1)
        def _():
            z_arrival(k, False).wait_recv()

    def stencil(k, z0):
        lane = pl.multiple_of(chunk(k) * LC, LC)
        slab = jnp.concatenate(
            [
                vp[z0 : z0 + ZB + 4, :, pl.ds(pl.multiple_of(lane + PAD, PAD), LC)].reshape((ZB + 4) * cx, LC),
                xhl[z0 * 2 : (z0 + ZB) * 2, pl.ds(lane, LC)],
                xhr[z0 * 2 : (z0 + ZB) * 2, pl.ds(lane, LC)],
                jnp.zeros((32, LC), jnp.bfloat16),
            ],
            axis=0,
        )
        return jnp.dot(dzx[...], slab, preferred_element_type=jnp.float32)

    wait_halo(0)
    gbuf[...] = stencil(0, 0)

    def after_halo(k, _):
        inner = pl.multiple_of(chunk(k) * LC + PAD, PAD)
        m0 = jnp.zeros((cx, LC), jnp.float32)
        m1 = m0
        m2 = m0
        g = gbuf
        after = jnp.minimum(k + 1, nc - 1)
        for z0 in range(0, nz, ZB):
            if z0 == nz // 2:

                @pl.when(k < nc - 1)
                def _():
                    wait_halo(after)

            ahead = stencil(k, z0 + ZB) if z0 + ZB < nz else stencil(after, 0)
            for j in range(ZB):
                here = slice((z0 + j) * cx, (z0 + j + 1) * cx)
                p = g[j * cx : (j + 1) * cx]
                q = g[128 + j * cx : 128 + (j + 1) * cx]
                facing = jnp.abs(p + gy2[k, here])
                facing = facing * lax.rsqrt(p * p + q * q + gyq[k, here])
                w = wt[k, here] * (facing + BASE)
                f = vp[2 + z0 + j, :, pl.ds(inner, LC)].astype(jnp.float32)
                wf = w * f
                m0 = m0 + w
                m1 = m1 + wf
                m2 = m2 + wf * f
            g = ahead
        gbuf[...] = g
        s = ss[k]
        for q in range(per):
            part = slice((q // 2) * 128, (q // 2 + 1) * 128)
            a, b, c, e = m0[:, part], m1[:, part], m2[:, part], s[:, part]
            if q % 2 == 0:
                first = jnp.where(low, a, pltpu.roll(b, OW, 1))
                second = jnp.where(low, c, pltpu.roll(e, OW, 1))
            else:
                first = jnp.where(low, pltpu.roll(a, OW, 1), b)
                second = jnp.where(low, pltpu.roll(c, OW, 1), e)
            owner = chunk(k) * per + q

            @pl.when(owner != d)
            def _():
                sb[owner, 0] = encode(first)
                sb[owner, 1] = encode(second)
                send(owner).start()

            @pl.when(owner == d)
            def _():
                got[d, 0] = first
                got[d, 1] = second

        return 0

    lax.fori_loop(0, nc, after_halo, 0)

    def take(r, q):
        @pl.when((r != row) | (q != col))
        def _():
            i = r * per + q
            arrival(i).wait_recv()
            got[i] = decode(rb[i])

    def other_row(n, _):
        for q in range(per):
            take(lax.rem(row + n, nc), q)
        return 0

    lax.fori_loop(1, nc + 1, other_row, 0)
    ahead = jnp.zeros((cx, 128), jnp.float32)
    acc0 = ahead
    acc1 = ahead
    for i in range(nd):
        p0, p1 = got[i, 0], got[i, 1]
        through = jnp.exp2(-ahead)
        acc0 = acc0 + through * p0
        acc1 = acc1 + through * p1
        ahead = ahead + jnp.where(low, pltpu.roll(p1, OW, 1), p1)
    a = acc0 * GAIN
    b = pltpu.roll(a, OW, 1)
    c = acc1 * GAIN
    o_ref[0] = (a + 0.5 * b)[:, :OW]
    o_ref[1] = (a - 0.3 * b + 0.2 * c)[:, :OW]
    o_ref[2] = (a + 0.25 * b - 0.1 * c)[:, :OW]
    o_ref[3] = (1.0 - jnp.exp2(-ahead))[:, :OW]

    for k in range(nc):

        @pl.when(t < nt - 1)
        def _():
            x_up(k).wait_send()

        @pl.when(t > 0)
        def _():
            x_down(k).wait_send()

        @pl.when(d < nd - 1)
        def _():
            z_copy(k, True).wait_send()

        @pl.when(d > 0)
        def _():
            z_copy(k, False).wait_send()

    for i in range(nd):

        @pl.when(d != i)
        def _():
            send(i).wait_send()


def solution(mesh):
    nd, nt = mesh.shape["depth"], mesh.shape["tile"]

    def body(volume):
        nz, cx, ny = volume.shape
        nc = ny // LC
        big = (nc, nz * cx, LC)
        return pl.pallas_call(
            functools.partial(kernel, nd, nt),
            out_shape=jax.ShapeDtypeStruct((4, cx, OW), jnp.float32),
            in_specs=[pl.BlockSpec(memory_space=pl.ANY)],
            out_specs=pl.BlockSpec(memory_space=pltpu.VMEM),
            scratch_shapes=[
                pltpu.VMEM((nz + 4, cx, ny + 2 * PAD), jnp.bfloat16),
                pltpu.VMEM((nz * 2, ny), jnp.bfloat16),
                pltpu.VMEM((nz * 2, ny), jnp.bfloat16),
                pltpu.VMEM((nz * 2, ny), jnp.bfloat16),
                pltpu.VMEM((nz * 2, ny), jnp.bfloat16),
                pltpu.VMEM(big, jnp.float32),
                pltpu.VMEM(big, jnp.float32),
                pltpu.VMEM(big, jnp.float32),
                pltpu.VMEM((nc, cx, LC), jnp.float32),
                pltpu.VMEM((256, 256), jnp.bfloat16),
                pltpu.VMEM((LC + 2 * PAD, LC), jnp.bfloat16),
                pltpu.VMEM((nd, 2, cx, 128), jnp.bfloat16),
                pltpu.VMEM((nd, 2, cx, 128), jnp.bfloat16),
                pltpu.VMEM((nd, 2, cx, 128), jnp.float32),
                pltpu.VMEM((256, LC), jnp.float32),
                pltpu.SemaphoreType.DMA((nc,)),
                pltpu.SemaphoreType.DMA((2, nc)),
                pltpu.SemaphoreType.DMA((2, nc)),
                pltpu.SemaphoreType.DMA((2, nc)),
                pltpu.SemaphoreType.DMA((2, nc)),
                pltpu.SemaphoreType.DMA((nd,)),
                pltpu.SemaphoreType.DMA((nd,)),
            ],
            compiler_params=pltpu.CompilerParams(
                collective_id=0, has_side_effects=True, vmem_limit_bytes=60 * 2**20
            ),
        )(volume)

    return jax.shard_map(
        body,
        mesh=mesh,
        in_specs=(P("depth", "tile", None),),
        out_specs=P(None, "tile", "depth"),
        check_vma=False,
    )
```

```python
import functools
import math

import jax
import jax.numpy as jnp
from jax import lax
from jax.experimental import pallas as pl
from jax.experimental.pallas import tpu as pltpu
from jax.sharding import PartitionSpec as P

MESH = pl.DeviceIdType.MESH
LC = 256
OW = 64
ZB = 8
PAD = 128
BASE = 0.15 * 3.0 / 0.85 / math.sqrt(5.0)
CODE = 44.0
GAIN = 0.85 / 3.0 * math.sqrt(5.0)


def taps(delta):
    value = jnp.where(delta == -2, 1.0, 0.0)
    value = jnp.where(delta == -1, -8.0, value)
    value = jnp.where(delta == 1, 8.0, value)
    return jnp.where(delta == 2, -1.0, value)


def stencil_zx():
    out = lax.broadcasted_iota(jnp.int32, (128, 256), 0)
    col = lax.broadcasted_iota(jnp.int32, (128, 256), 1)
    zo, xo = out >> 4, out & 15
    zi, xi = (col >> 4) - 2, col & 15
    inside = col < 192
    gz = jnp.where(inside & (xi == xo), taps(zi - zo), 0.0)
    k = col & 15
    pos = (k & 1) + jnp.where(col >= 208, 16, -2)
    plane = jnp.where(inside, zi, jnp.where(col < 224, k >> 1, -9))
    gx = jnp.where(plane == zo, taps(jnp.where(inside, xi, pos) - xo), 0.0)
    return gx + 2.0 * gz, 2.0 * gx - gz


def encode(value):
    v = value * CODE
    v2 = v * v
    v4 = v2 * v2
    return (v4 * v4 * v2 * v).astype(jnp.bfloat16)


def decode(code):
    u = code.astype(jnp.float32)
    size = jnp.exp2(jnp.log2(jnp.maximum(jnp.abs(u), 1e-37)) * (1.0 / 11.0) - math.log2(CODE))
    return jnp.where(u < 0.0, -size, size)


def kernel(nd, nt, v_ref, o_ref, vp, xhl, xhr, elo, ehi, gy2, gyq, wt, ss, dzx, dy,
           sb, rb, got, gbuf, load_sem, zs, zr, xs, xr, cs, cr):
    nz, cx, ny = v_ref.shape
    nc = ny // LC
    per = LC // OW
    d = lax.axis_index("depth")
    t = lax.axis_index("tile")
    row, col = d // per, lax.rem(d, per)
    scale = math.log2(math.e) / (nz * nd)

    def chunk(k, r=None):
        r = row if r is None else r
        if nc != 4:
            return lax.rem(r + 1 + k, nc)
        if isinstance(k, int):
            return lax.rem(r + (2, 1, 3, 0)[k], nc)
        return lax.rem(r + jnp.where(k == 3, 0, jnp.where(k == 2, 3, 2 - k)), nc)

    def load(k):
        lane = pl.multiple_of(chunk(k) * LC, LC)
        return pltpu.make_async_copy(
            v_ref.at[:, :, pl.ds(lane, LC)],
            vp.at[pl.ds(2, nz), :, pl.ds(pl.multiple_of(lane + PAD, PAD), LC)],
            load_sem.at[k],
        )

    for k in range(nc):
        load(k).start()

    barrier = pltpu.get_barrier_semaphore()

    def greet(depth, tile):
        pl.semaphore_signal(barrier, inc=1, device_id=(depth, tile), device_id_type=MESH)

    @pl.when(t > 0)
    def _():
        greet(d, t - 1)

    @pl.when(t < nt - 1)
    def _():
        greet(d, t + 1)

    for i in (1, nd - 1, *range(2, nd - 1)):
        greet(lax.rem(d + i, nd), t)

    zeros = jnp.zeros((nz, cx, PAD), jnp.bfloat16)
    vp[2 : 2 + nz, :, 0:PAD] = zeros
    vp[2 : 2 + nz, :, PAD + ny :] = zeros

    @pl.when(d == 0)
    def _():
        vp[0:2] = jnp.zeros((2, cx, ny + 2 * PAD), jnp.bfloat16)

    @pl.when(d == nd - 1)
    def _():
        vp[nz + 2 :] = jnp.zeros((2, cx, ny + 2 * PAD), jnp.bfloat16)

    @pl.when(t == 0)
    def _():
        xhl[...] = jnp.zeros(xhl.shape, jnp.bfloat16)

    @pl.when(t == nt - 1)
    def _():
        xhr[...] = jnp.zeros(xhr.shape, jnp.bfloat16)

    p_taps, q_taps = stencil_zx()
    dzx[0:128] = p_taps.astype(jnp.bfloat16)
    dzx[128:256] = q_taps.astype(jnp.bfloat16)
    src = lax.broadcasted_iota(jnp.int32, (PAD, LC), 0)
    dst = lax.broadcasted_iota(jnp.int32, (PAD, LC), 1)
    for i in range(0, LC + 2 * PAD, PAD):
        dy[i : i + PAD] = (2.0 * taps(src - dst + (i - PAD))).astype(jnp.bfloat16)

    def z_copy(k, up):
        there = lax.rem(d + (1 if up else nd - 1), nd)
        lane = pl.multiple_of(chunk(k, there // per) * LC, LC)
        return pltpu.make_async_remote_copy(
            src_ref=v_ref.at[pl.ds(nz - 2 if up else 0, 2), :, pl.ds(lane, LC)],
            dst_ref=vp.at[pl.ds(0 if up else nz + 2, 2), :, pl.ds(pl.multiple_of(lane + PAD, PAD), LC)],
            send_sem=zs.at[1 - up, k], recv_sem=zr.at[1 - up, k],
            device_id=(there, t), device_id_type=MESH,
        )

    def z_arrival(k, up):
        lane = pl.multiple_of(chunk(k) * LC, LC)
        return pltpu.make_async_remote_copy(
            src_ref=v_ref.at[pl.ds(0, 2), :, pl.ds(lane, LC)],
            dst_ref=vp.at[pl.ds(0 if up else nz + 2, 2), :, pl.ds(pl.multiple_of(lane + PAD, PAD), LC)],
            send_sem=zs.at[1 - up, k], recv_sem=zr.at[1 - up, k],
            device_id=(d, t), device_id_type=MESH,
        )

    def x_up(k):
        lane = pl.ds(pl.multiple_of(chunk(k) * LC, LC), LC)
        return pltpu.make_async_remote_copy(
            src_ref=ehi.at[:, lane], dst_ref=xhl.at[:, lane],
            send_sem=xs.at[0, k], recv_sem=xr.at[0, k],
            device_id=(d, lax.rem(t + 1, nt)), device_id_type=MESH,
        )

    def x_down(k):
        lane = pl.ds(pl.multiple_of(chunk(k) * LC, LC), LC)
        return pltpu.make_async_remote_copy(
            src_ref=elo.at[:, lane], dst_ref=xhr.at[:, lane],
            send_sem=xs.at[1, k], recv_sem=xr.at[1, k],
            device_id=(d, lax.rem(t + nt - 1, nt)), device_id_type=MESH,
        )

    for k in range(nc):
        load(k).wait()
        lane = pl.multiple_of(chunk(k) * LC, LC)
        rows = vp[2 : 2 + nz, :, pl.ds(pl.multiple_of(lane + PAD, PAD), LC)]
        elo[:, pl.ds(lane, LC)] = rows[:, 0:2].reshape(nz * 2, LC)
        ehi[:, pl.ds(lane, LC)] = rows[:, cx - 2 : cx].reshape(nz * 2, LC)
        if k == 0:
            waits = nd - 1 + (t > 0).astype(jnp.int32) + (t < nt - 1).astype(jnp.int32)
            pl.semaphore_wait(barrier, waits)

        @pl.when(t < nt - 1)
        def _():
            x_up(k).start()

        @pl.when(t > 0)
        def _():
            x_down(k).start()

        @pl.when(d < nd - 1)
        def _():
            z_copy(k, True).start()

        @pl.when(d > 0)
        def _():
            z_copy(k, False).start()

    def before_halo(k, _):
        lane = pl.multiple_of(chunk(k) * LC, LC)
        total = jnp.zeros((cx, LC), jnp.float32)
        last = jnp.ones((cx, LC), jnp.float32)
        part = min(256 // cx, nz)
        for z0 in range(0, nz, part):
            slab = vp[2 + z0 : 2 + z0 + part, :, pl.ds(lane, LC + 2 * PAD)]
            slab = slab.reshape(part * cx, LC + 2 * PAD)
            g = jnp.dot(slab, dy[...], preferred_element_type=jnp.float32)
            gy2[k, z0 * cx : (z0 + part) * cx] = g
            gyq[k, z0 * cx : (z0 + part) * cx] = g * g * 1.25 + 720.0
            for z in range(z0, z0 + part):
                f = vp[2 + z, :, pl.ds(pl.multiple_of(lane + PAD, PAD), LC)].astype(jnp.float32)
                total = total + f * f
                now = jnp.exp2(total * -scale - scale * (z + 1))
                wt[k, z * cx : (z + 1) * cx] = last - now
                last = now
        ss[k] = total * scale + scale * nz
        return 0

    lax.fori_loop(0, nc, before_halo, 0)

    low = lax.broadcasted_iota(jnp.int32, (cx, 128), 1) < OW

    def send(owner):
        return pltpu.make_async_remote_copy(
            src_ref=sb.at[owner], dst_ref=rb.at[d],
            send_sem=cs.at[owner], recv_sem=cr.at[d],
            device_id=(owner, t), device_id_type=MESH,
        )

    def arrival(i):
        return pltpu.make_async_remote_copy(
            src_ref=sb.at[i], dst_ref=rb.at[i],
            send_sem=cs.at[i], recv_sem=cr.at[i],
            device_id=(d, t), device_id_type=MESH,
        )

    def wait_halo(k):
        @pl.when(t > 0)
        def _():
            x_up(k).wait_recv()

        @pl.when(t < nt - 1)
        def _():
            x_down(k).wait_recv()

        @pl.when(d > 0)
        def _():
            z_arrival(k, True).wait_recv()

        @pl.when(d < nd - 1)
        def _():
            z_arrival(k, False).wait_recv()

    def stencil(k, z0):
        lane = pl.multiple_of(chunk(k) * LC, LC)
        slab = jnp.concatenate(
            [
                vp[z0 : z0 + ZB + 4, :, pl.ds(pl.multiple_of(lane + PAD, PAD), LC)].reshape((ZB + 4) * cx, LC),
                xhl[z0 * 2 : (z0 + ZB) * 2, pl.ds(lane, LC)],
                xhr[z0 * 2 : (z0 + ZB) * 2, pl.ds(lane, LC)],
                jnp.zeros((32, LC), jnp.bfloat16),
            ],
            axis=0,
        )
        return jnp.dot(dzx[...], slab, preferred_element_type=jnp.float32)

    wait_halo(0)
    gbuf[...] = stencil(0, 0)

    def after_halo(k, _):
        inner = pl.multiple_of(chunk(k) * LC + PAD, PAD)
        m0 = jnp.zeros((cx, LC), jnp.float32)
        m1 = m0
        m2 = m0
        g = gbuf
        after = jnp.minimum(k + 1, nc - 1)

        @pl.when(k < nc - 1)
        def _():
            wait_halo(after)

        for z0 in range(0, nz, ZB):
            ahead = stencil(k, z0 + ZB) if z0 + ZB < nz else stencil(after, 0)
            for j in range(ZB):
                here = slice((z0 + j) * cx, (z0 + j + 1) * cx)
                p = g[j * cx : (j + 1) * cx]
                q = g[128 + j * cx : 128 + (j + 1) * cx]
                facing = jnp.abs(p + gy2[k, here])
                facing = facing * lax.rsqrt(p * p + q * q + gyq[k, here])
                w = wt[k, here] * (facing + BASE)
                f = vp[2 + z0 + j, :, pl.ds(inner, LC)].astype(jnp.float32)
                wf = w * f
                m0 = m0 + w
                m1 = m1 + wf
                m2 = m2 + wf * f
            g = ahead
        gbuf[...] = g
        s = ss[k]
        for q in range(per):
            part = slice((q // 2) * 128, (q // 2 + 1) * 128)
            a, b, c, e = m0[:, part], m1[:, part], m2[:, part], s[:, part]
            if q % 2 == 0:
                first = jnp.where(low, a, pltpu.roll(b, OW, 1))
                second = jnp.where(low, c, pltpu.roll(e, OW, 1))
            else:
                first = jnp.where(low, pltpu.roll(a, OW, 1), b)
                second = jnp.where(low, pltpu.roll(c, OW, 1), e)
            owner = chunk(k) * per + q

            @pl.when(owner != d)
            def _():
                sb[owner, 0] = encode(first)
                sb[owner, 1] = encode(second)
                send(owner).start()

            @pl.when(owner == d)
            def _():
                got[d, 0] = first
                got[d, 1] = second

        return 0

    lax.fori_loop(0, nc, after_halo, 0)

    def take(r, q):
        @pl.when((r != row) | (q != col))
        def _():
            i = r * per + q
            arrival(i).wait_recv()
            got[i] = decode(rb[i])

    def other_row(n, _):
        for q in range(per):
            take(lax.rem(row + n, nc), q)
        return 0

    lax.fori_loop(1, nc + 1, other_row, 0)
    ahead = jnp.zeros((cx, 128), jnp.float32)
    acc0 = ahead
    acc1 = ahead
    for i in range(nd):
        p0, p1 = got[i, 0], got[i, 1]
        through = jnp.exp2(-ahead)
        acc0 = acc0 + through * p0
        acc1 = acc1 + through * p1
        ahead = ahead + jnp.where(low, pltpu.roll(p1, OW, 1), p1)
    a = acc0 * GAIN
    b = pltpu.roll(a, OW, 1)
    c = acc1 * GAIN
    o_ref[0] = (a + 0.5 * b)[:, :OW]
    o_ref[1] = (a - 0.3 * b + 0.2 * c)[:, :OW]
    o_ref[2] = (a + 0.25 * b - 0.1 * c)[:, :OW]
    o_ref[3] = (1.0 - jnp.exp2(-ahead))[:, :OW]

    for k in range(nc):

        @pl.when(t < nt - 1)
        def _():
            x_up(k).wait_send()

        @pl.when(t > 0)
        def _():
            x_down(k).wait_send()

        @pl.when(d < nd - 1)
        def _():
            z_copy(k, True).wait_send()

        @pl.when(d > 0)
        def _():
            z_copy(k, False).wait_send()

    for i in range(nd):

        @pl.when(d != i)
        def _():
            send(i).wait_send()


def solution(mesh):
    nd, nt = mesh.shape["depth"], mesh.shape["tile"]

    def body(volume):
        nz, cx, ny = volume.shape
        nc = ny // LC
        big = (nc, nz * cx, LC)
        return pl.pallas_call(
            functools.partial(kernel, nd, nt),
            out_shape=jax.ShapeDtypeStruct((4, cx, OW), jnp.float32),
            in_specs=[pl.BlockSpec(memory_space=pl.ANY)],
            out_specs=pl.BlockSpec(memory_space=pltpu.VMEM),
            scratch_shapes=[
                pltpu.VMEM((nz + 4, cx, ny + 2 * PAD), jnp.bfloat16),
                pltpu.VMEM((nz * 2, ny), jnp.bfloat16),
                pltpu.VMEM((nz * 2, ny), jnp.bfloat16),
                pltpu.VMEM((nz * 2, ny), jnp.bfloat16),
                pltpu.VMEM((nz * 2, ny), jnp.bfloat16),
                pltpu.VMEM(big, jnp.float32),
                pltpu.VMEM(big, jnp.float32),
                pltpu.VMEM(big, jnp.float32),
                pltpu.VMEM((nc, cx, LC), jnp.float32),
                pltpu.VMEM((256, 256), jnp.bfloat16),
                pltpu.VMEM((LC + 2 * PAD, LC), jnp.bfloat16),
                pltpu.VMEM((nd, 2, cx, 128), jnp.bfloat16),
                pltpu.VMEM((nd, 2, cx, 128), jnp.bfloat16),
                pltpu.VMEM((nd, 2, cx, 128), jnp.float32),
                pltpu.VMEM((256, LC), jnp.float32),
                pltpu.SemaphoreType.DMA((nc,)),
                pltpu.SemaphoreType.DMA((2, nc)),
                pltpu.SemaphoreType.DMA((2, nc)),
                pltpu.SemaphoreType.DMA((2, nc)),
                pltpu.SemaphoreType.DMA((2, nc)),
                pltpu.SemaphoreType.DMA((nd,)),
                pltpu.SemaphoreType.DMA((nd,)),
            ],
            compiler_params=pltpu.CompilerParams(
                collective_id=0, has_side_effects=True, vmem_limit_bytes=105 * 2**19
            ),
        )(volume)

    return jax.shard_map(
        body,
        mesh=mesh,
        in_specs=(P("depth", "tile", None),),
        out_specs=P(None, "tile", "depth"),
        check_vma=False,
    )
```

```python
import functools
import math

import jax
import jax.numpy as jnp
from jax import lax
from jax.experimental import pallas as pl
from jax.experimental.pallas import tpu as pltpu
from jax.sharding import PartitionSpec as P

MESH = pl.DeviceIdType.MESH
LC = 256
OW = 64
ZB = 8
PAD = 128
BASE = 0.15 * 3.0 / 0.85 / math.sqrt(5.0)
CODE = 44.0
GAIN = 0.85 / 3.0 * math.sqrt(5.0)


def taps(delta):
    value = jnp.where(delta == -2, 1.0, 0.0)
    value = jnp.where(delta == -1, -8.0, value)
    value = jnp.where(delta == 1, 8.0, value)
    return jnp.where(delta == 2, -1.0, value)


def stencil_zx():
    out = lax.broadcasted_iota(jnp.int32, (128, 256), 0)
    col = lax.broadcasted_iota(jnp.int32, (128, 256), 1)
    zo, xo = out >> 4, out & 15
    zi, xi = (col >> 4) - 2, col & 15
    inside = col < 192
    gz = jnp.where(inside & (xi == xo), taps(zi - zo), 0.0)
    k = col & 15
    pos = (k & 1) + jnp.where(col >= 208, 16, -2)
    plane = jnp.where(inside, zi, jnp.where(col < 224, k >> 1, -9))
    gx = jnp.where(plane == zo, taps(jnp.where(inside, xi, pos) - xo), 0.0)
    return gx + 2.0 * gz, 2.0 * gx - gz


def encode(value):
    v = value * CODE
    v2 = v * v
    v4 = v2 * v2
    return (v4 * v4 * v2 * v).astype(jnp.bfloat16)


def decode(code):
    u = code.astype(jnp.float32)
    size = jnp.exp2(jnp.log2(jnp.maximum(jnp.abs(u), 1e-37)) * (1.0 / 11.0) - math.log2(CODE))
    return jnp.where(u < 0.0, -size, size)


def kernel(nd, nt, v_ref, o_ref, vp, xhl, xhr, elo, ehi, gy2, gyq, wt, wt1, wt2, ss, dzx, dy,
           sb, rb, got, load_sem, zs, zr, xs, xr, cs, cr, ready):
    nz, cx, ny = v_ref.shape
    nc = ny // LC
    per = LC // OW
    d = lax.axis_index("depth")
    t = lax.axis_index("tile")
    row, col = d // per, lax.rem(d, per)
    scale = math.log2(math.e) / (nz * nd)

    def chunk(k, r=None):
        r = row if r is None else r
        if nc != 4:
            return lax.rem(r + 1 + k, nc)
        if isinstance(k, int):
            return lax.rem(r + (2, 1, 3, 0)[k], nc)
        return lax.rem(r + jnp.where(k == 3, 0, jnp.where(k == 2, 3, 2 - k)), nc)

    def load(k):
        lane = pl.multiple_of(chunk(k) * LC, LC)
        return pltpu.make_async_copy(
            v_ref.at[:, :, pl.ds(lane, LC)],
            vp.at[pl.ds(2, nz), :, pl.ds(pl.multiple_of(lane + PAD, PAD), LC)],
            load_sem.at[k],
        )

    for k in range(nc):
        load(k).start()

    barrier = pltpu.get_barrier_semaphore()

    def greet(depth, tile):
        pl.semaphore_signal(barrier, inc=1, device_id=(depth, tile), device_id_type=MESH)

    @pl.when(t > 0)
    def _():
        greet(d, t - 1)

    @pl.when(t < nt - 1)
    def _():
        greet(d, t + 1)

    crosses_up = (col == per - 1) & (d < nd - 1)
    crosses_down = (col == 0) & (d > 0)

    @pl.when(crosses_up)
    def _():
        greet(d + 1, t)

    @pl.when(crosses_down)
    def _():
        greet(d - 1, t)

    for i in range(1, per):
        greet(row * per + lax.rem(col + i, per), t)
    for i in range(1, nc):
        greet(lax.rem(row + i, nc) * per + col, t)

    zeros = jnp.zeros((nz, cx, PAD), jnp.bfloat16)
    vp[2 : 2 + nz, :, 0:PAD] = zeros
    vp[2 : 2 + nz, :, PAD + ny :] = zeros

    @pl.when(d == 0)
    def _():
        vp[0:2] = jnp.zeros((2, cx, ny + 2 * PAD), jnp.bfloat16)

    @pl.when(d == nd - 1)
    def _():
        vp[nz + 2 :] = jnp.zeros((2, cx, ny + 2 * PAD), jnp.bfloat16)

    @pl.when(t == 0)
    def _():
        xhl[...] = jnp.zeros(xhl.shape, jnp.bfloat16)

    @pl.when(t == nt - 1)
    def _():
        xhr[...] = jnp.zeros(xhr.shape, jnp.bfloat16)

    p_taps, q_taps = stencil_zx()
    dzx[0:128] = p_taps.astype(jnp.bfloat16)
    dzx[128:256] = q_taps.astype(jnp.bfloat16)
    src = lax.broadcasted_iota(jnp.int32, (PAD, LC), 0)
    dst = lax.broadcasted_iota(jnp.int32, (PAD, LC), 1)
    for i in range(0, LC + 2 * PAD, PAD):
        dy[i : i + PAD] = (2.0 * taps(src - dst + (i - PAD))).astype(jnp.bfloat16)

    def z_copy(k, up):
        there = lax.rem(d + (1 if up else nd - 1), nd)
        lane = pl.multiple_of(chunk(k, there // per) * LC, LC)
        return pltpu.make_async_remote_copy(
            src_ref=v_ref.at[pl.ds(nz - 2 if up else 0, 2), :, pl.ds(lane, LC)],
            dst_ref=vp.at[pl.ds(0 if up else nz + 2, 2), :, pl.ds(pl.multiple_of(lane + PAD, PAD), LC)],
            send_sem=zs.at[1 - up, k], recv_sem=zr.at[1 - up, k],
            device_id=(there, t), device_id_type=MESH,
        )

    def z_arrival(k, up):
        lane = pl.multiple_of(chunk(k) * LC, LC)
        return pltpu.make_async_remote_copy(
            src_ref=v_ref.at[pl.ds(0, 2), :, pl.ds(lane, LC)],
            dst_ref=vp.at[pl.ds(0 if up else nz + 2, 2), :, pl.ds(pl.multiple_of(lane + PAD, PAD), LC)],
            send_sem=zs.at[1 - up, k], recv_sem=zr.at[1 - up, k],
            device_id=(d, t), device_id_type=MESH,
        )

    def x_up(k):
        return pltpu.make_async_remote_copy(
            src_ref=ehi.at[k], dst_ref=xhl.at[k],
            send_sem=xs.at[0, k], recv_sem=xr.at[0, k],
            device_id=(d, lax.rem(t + 1, nt)), device_id_type=MESH,
        )

    def x_down(k):
        return pltpu.make_async_remote_copy(
            src_ref=elo.at[k], dst_ref=xhr.at[k],
            send_sem=xs.at[1, k], recv_sem=xr.at[1, k],
            device_id=(d, lax.rem(t + nt - 1, nt)), device_id_type=MESH,
        )

    for k in range(nc):
        load(k).wait()
        lane = pl.multiple_of(chunk(k) * LC, LC)
        rows = vp[2 : 2 + nz, :, pl.ds(pl.multiple_of(lane + PAD, PAD), LC)]
        elo[k] = rows[:, 0:2].reshape(nz * 2, LC)
        ehi[k] = rows[:, cx - 2 : cx].reshape(nz * 2, LC)
        if k == 0:
            waits = per - 1 + nc - 1
            for there in (t > 0, t < nt - 1, crosses_up, crosses_down):
                waits = waits + there.astype(jnp.int32)
            pl.semaphore_wait(barrier, waits)

        @pl.when(t < nt - 1)
        def _():
            x_up(k).start()

        @pl.when(t > 0)
        def _():
            x_down(k).start()

        @pl.when(d < nd - 1)
        def _():
            z_copy(k, True).start()

        @pl.when(d > 0)
        def _():
            z_copy(k, False).start()

    for i in range(1, nc):
        pl.semaphore_signal(
            ready, inc=1, device_id=(lax.rem(row + i, nc) * per + col, t), device_id_type=MESH
        )

    def before_halo(k, _):
        lane = pl.multiple_of(chunk(k) * LC, LC)
        total = jnp.zeros((cx, LC), jnp.float32)
        last = jnp.ones((cx, LC), jnp.float32)
        sum1 = total
        sum2 = total
        part = min(256 // cx, nz)
        for z0 in range(0, nz, part):
            slab = vp[2 + z0 : 2 + z0 + part, :, pl.ds(lane, LC + 2 * PAD)]
            slab = slab.reshape(part * cx, LC + 2 * PAD)
            g = jnp.dot(slab, dy[...], preferred_element_type=jnp.float32)
            gy2[k, z0 * cx : (z0 + part) * cx] = g
            gyq[k, z0 * cx : (z0 + part) * cx] = g * g * 1.25 + 720.0
            for z in range(z0, z0 + part):
                f = vp[2 + z, :, pl.ds(pl.multiple_of(lane + PAD, PAD), LC)].astype(jnp.float32)
                ff = f * f
                total = total + ff
                now = jnp.exp2(total * -scale - scale * (z + 1))
                w = last - now
                wf = w * f
                wff = w * ff
                here = slice(z * cx, (z + 1) * cx)
                wt[k, here] = w
                wt1[k, here] = wf
                wt2[k, here] = wff
                sum1 = sum1 + wf
                sum2 = sum2 + wff
                last = now
        ss[k, 0] = BASE * (1.0 - last)
        ss[k, 1] = BASE * sum1
        ss[k, 2] = BASE * sum2
        ss[k, 3] = total * scale + scale * nz
        return 0

    lax.fori_loop(0, nc, before_halo, 0)
    pl.semaphore_wait(ready, nc - 1)

    low = lax.broadcasted_iota(jnp.int32, (cx, 128), 1) < OW

    def send(owner):
        return pltpu.make_async_remote_copy(
            src_ref=sb.at[owner], dst_ref=rb.at[d],
            send_sem=cs.at[owner], recv_sem=cr.at[d],
            device_id=(owner, t), device_id_type=MESH,
        )

    def arrival(i):
        return pltpu.make_async_remote_copy(
            src_ref=sb.at[i], dst_ref=rb.at[i],
            send_sem=cs.at[i], recv_sem=cr.at[i],
            device_id=(d, t), device_id_type=MESH,
        )

    def wait_halo(k):
        @pl.when(t > 0)
        def _():
            x_up(k).wait_recv()

        @pl.when(t < nt - 1)
        def _():
            x_down(k).wait_recv()

        @pl.when(d > 0)
        def _():
            z_arrival(k, True).wait_recv()

        @pl.when(d < nd - 1)
        def _():
            z_arrival(k, False).wait_recv()

    def stencil(k, z0):
        lane = pl.multiple_of(chunk(k) * LC, LC)
        slab = jnp.concatenate(
            [
                vp[z0 : z0 + ZB + 4, :, pl.ds(pl.multiple_of(lane + PAD, PAD), LC)].reshape((ZB + 4) * cx, LC),
                xhl[k, z0 * 2 : (z0 + ZB) * 2],
                xhr[k, z0 * 2 : (z0 + ZB) * 2],
                jnp.zeros((32, LC), jnp.bfloat16),
            ],
            axis=0,
        )
        return jnp.dot(dzx[...], slab, preferred_element_type=jnp.float32)

    def after_halo(k, _):
        m0, m1, m2 = ss[k, 0], ss[k, 1], ss[k, 2]
        wait_halo(k)
        for z0 in range(0, nz, ZB):
            g = stencil(k, z0)
            for j in range(ZB):
                here = slice((z0 + j) * cx, (z0 + j + 1) * cx)
                p = g[j * cx : (j + 1) * cx]
                q = g[128 + j * cx : 128 + (j + 1) * cx]
                facing = jnp.abs(p + gy2[k, here])
                facing = facing * lax.rsqrt(p * p + q * q + gyq[k, here])
                m0 = m0 + facing * wt[k, here]
                m1 = m1 + facing * wt1[k, here]
                m2 = m2 + facing * wt2[k, here]
        s = ss[k, 3]
        for q in range(per):
            part = slice((q // 2) * 128, (q // 2 + 1) * 128)
            a, b, c, e = m0[:, part], m1[:, part], m2[:, part], s[:, part]
            if q % 2 == 0:
                first = jnp.where(low, a, pltpu.roll(b, OW, 1))
                second = jnp.where(low, c, pltpu.roll(e, OW, 1))
            else:
                first = jnp.where(low, pltpu.roll(a, OW, 1), b)
                second = jnp.where(low, pltpu.roll(c, OW, 1), e)
            owner = chunk(k) * per + q

            @pl.when(owner != d)
            def _():
                sb[owner, 0] = encode(first)
                sb[owner, 1] = encode(second)
                send(owner).start()

            @pl.when(owner == d)
            def _():
                got[d, 0] = first
                got[d, 1] = second

        return 0

    lax.fori_loop(0, nc, after_halo, 0)

    def take(r, q):
        @pl.when((r != row) | (q != col))
        def _():
            i = r * per + q
            arrival(i).wait_recv()
            got[i] = decode(rb[i])

    def other_row(n, _):
        for q in range(per):
            take(lax.rem(row + n, nc), q)
        return 0

    lax.fori_loop(1, nc, other_row, 0)
    for k in range(nc):

        @pl.when(t < nt - 1)
        def _():
            x_up(k).wait_send()

        @pl.when(t > 0)
        def _():
            x_down(k).wait_send()

        @pl.when(d < nd - 1)
        def _():
            z_copy(k, True).wait_send()

        @pl.when(d > 0)
        def _():
            z_copy(k, False).wait_send()

    for i in range(nd):

        @pl.when(d != i)
        def _():
            send(i).wait_send()
    for q in range(per):
        take(row, q)
    ahead = jnp.zeros((cx, 128), jnp.float32)
    acc0 = ahead
    acc1 = ahead
    for i in range(nd):
        p0, p1 = got[i, 0], got[i, 1]
        through = jnp.exp2(-ahead)
        acc0 = acc0 + through * p0
        acc1 = acc1 + through * p1
        ahead = ahead + jnp.where(low, pltpu.roll(p1, OW, 1), p1)
    a = acc0 * GAIN
    b = pltpu.roll(a, OW, 1)
    c = acc1 * GAIN
    o_ref[0] = (a + 0.5 * b)[:, :OW]
    o_ref[1] = (a - 0.3 * b + 0.2 * c)[:, :OW]
    o_ref[2] = (a + 0.25 * b - 0.1 * c)[:, :OW]
    o_ref[3] = (1.0 - jnp.exp2(-ahead))[:, :OW]


def solution(mesh):
    nd, nt = mesh.shape["depth"], mesh.shape["tile"]

    def body(volume):
        nz, cx, ny = volume.shape
        nc = ny // LC
        big = (nc, nz * cx, LC)
        return pl.pallas_call(
            functools.partial(kernel, nd, nt),
            out_shape=jax.ShapeDtypeStruct((4, cx, OW), jnp.float32),
            in_specs=[pl.BlockSpec(memory_space=pl.ANY)],
            out_specs=pl.BlockSpec(memory_space=pltpu.VMEM),
            scratch_shapes=[
                pltpu.VMEM((nz + 4, cx, ny + 2 * PAD), jnp.bfloat16),
                pltpu.VMEM((nc, nz * 2, LC), jnp.bfloat16),
                pltpu.VMEM((nc, nz * 2, LC), jnp.bfloat16),
                pltpu.VMEM((nc, nz * 2, LC), jnp.bfloat16),
                pltpu.VMEM((nc, nz * 2, LC), jnp.bfloat16),
                pltpu.VMEM(big, jnp.float32),
                pltpu.VMEM(big, jnp.float32),
                pltpu.VMEM(big, jnp.float32),
                pltpu.VMEM(big, jnp.float32),
                pltpu.VMEM(big, jnp.float32),
                pltpu.VMEM((nc, 4, cx, LC), jnp.float32),
                pltpu.VMEM((256, 256), jnp.bfloat16),
                pltpu.VMEM((LC + 2 * PAD, LC), jnp.bfloat16),
                pltpu.VMEM((nd, 2, cx, 128), jnp.bfloat16),
                pltpu.VMEM((nd, 2, cx, 128), jnp.bfloat16),
                pltpu.VMEM((nd, 2, cx, 128), jnp.float32),
                pltpu.SemaphoreType.DMA((nc,)),
                pltpu.SemaphoreType.DMA((2, nc)),
                pltpu.SemaphoreType.DMA((2, nc)),
                pltpu.SemaphoreType.DMA((2, nc)),
                pltpu.SemaphoreType.DMA((2, nc)),
                pltpu.SemaphoreType.DMA((nd,)),
                pltpu.SemaphoreType.DMA((nd,)),
                pltpu.SemaphoreType.REGULAR,
            ],
            compiler_params=pltpu.CompilerParams(
                collective_id=0, has_side_effects=True, vmem_limit_bytes=105 * 2**19
            ),
        )(volume)

    return jax.shard_map(
        body,
        mesh=mesh,
        in_specs=(P("depth", "tile", None),),
        out_specs=P(None, "tile", "depth"),
        check_vma=False,
    )
```

```python
import functools
import math

import jax
import jax.numpy as jnp
from jax import lax
from jax.experimental import pallas as pl
from jax.experimental.pallas import tpu as pltpu
from jax.sharding import PartitionSpec as P

MESH = pl.DeviceIdType.MESH
LC = 256
OW = 64
ZB = 8
PAD = 128
BASE = 0.15 * 3.0 / 0.85 / math.sqrt(5.0)
CODE = 44.0
GAIN = 0.85 / 3.0 * math.sqrt(5.0)


def taps(delta):
    value = jnp.where(delta == -2, 1.0, 0.0)
    value = jnp.where(delta == -1, -8.0, value)
    value = jnp.where(delta == 1, 8.0, value)
    return jnp.where(delta == 2, -1.0, value)


def stencil_zx():
    out = lax.broadcasted_iota(jnp.int32, (128, 256), 0)
    col = lax.broadcasted_iota(jnp.int32, (128, 256), 1)
    zo, xo = out >> 4, out & 15
    zi, xi = (col >> 4) - 2, col & 15
    inside = col < 192
    gz = jnp.where(inside & (xi == xo), taps(zi - zo), 0.0)
    k = col & 15
    pos = (k & 1) + jnp.where(col >= 208, 16, -2)
    plane = jnp.where(inside, zi, jnp.where(col < 224, k >> 1, -9))
    gx = jnp.where(plane == zo, taps(jnp.where(inside, xi, pos) - xo), 0.0)
    return gx + 2.0 * gz, 2.0 * gx - gz


def encode(value):
    v = value * CODE
    v2 = v * v
    v4 = v2 * v2
    return (v4 * v4 * v2 * v).astype(jnp.bfloat16)


def decode(code):
    u = code.astype(jnp.float32)
    size = jnp.exp2(jnp.log2(jnp.maximum(jnp.abs(u), 1e-37)) * (1.0 / 11.0) - math.log2(CODE))
    return jnp.where(u < 0.0, -size, size)


def kernel(nd, nt, v_ref, o_ref, vp, xhl, xhr, elo, ehi, gy2, gyq, wt, wt1, wt2, ss, dzx, dy,
           sb, rb, got, load_sem, zs, zr, xs, xr, cs, cr, ready):
    nz, cx, ny = v_ref.shape
    nc = ny // LC
    per = LC // OW
    d = lax.axis_index("depth")
    t = lax.axis_index("tile")
    row, col = d // per, lax.rem(d, per)
    scale = math.log2(math.e) / (nz * nd)

    barrier = pltpu.get_barrier_semaphore()

    def greet(depth, tile):
        pl.semaphore_signal(barrier, inc=1, device_id=(depth, tile), device_id_type=MESH)

    for i in range(1, per):
        greet(row * per + lax.rem(col + i, per), t)

    @pl.when(t > 0)
    def _():
        greet(d, t - 1)

    @pl.when(t < nt - 1)
    def _():
        greet(d, t + 1)

    crosses_up = (col == per - 1) & (d < nd - 1)
    crosses_down = (col == 0) & (d > 0)

    @pl.when(crosses_up)
    def _():
        greet(d + 1, t)

    @pl.when(crosses_down)
    def _():
        greet(d - 1, t)

    def chunk(k, r=None):
        r = row if r is None else r
        if nc != 4:
            return lax.rem(r + 1 + k, nc)
        if isinstance(k, int):
            return lax.rem(r + (2, 1, 3, 0)[k], nc)
        return lax.rem(r + jnp.where(k == 3, 0, jnp.where(k == 2, 3, 2 - k)), nc)

    def load(k):
        lane = pl.multiple_of(chunk(k) * LC, LC)
        return pltpu.make_async_copy(
            v_ref.at[:, :, pl.ds(lane, LC)],
            vp.at[pl.ds(2, nz), :, pl.ds(pl.multiple_of(lane + PAD, PAD), LC)],
            load_sem.at[k],
        )

    for k in range(nc):
        load(k).start()

    for i in range(1, nc):
        greet(lax.rem(row + i, nc) * per + col, t)

    zeros = jnp.zeros((nz, cx, PAD), jnp.bfloat16)
    vp[2 : 2 + nz, :, 0:PAD] = zeros
    vp[2 : 2 + nz, :, PAD + ny :] = zeros

    @pl.when(d == 0)
    def _():
        vp[0:2] = jnp.zeros((2, cx, ny + 2 * PAD), jnp.bfloat16)

    @pl.when(d == nd - 1)
    def _():
        vp[nz + 2 :] = jnp.zeros((2, cx, ny + 2 * PAD), jnp.bfloat16)

    @pl.when(t == 0)
    def _():
        xhl[...] = jnp.zeros(xhl.shape, jnp.bfloat16)

    @pl.when(t == nt - 1)
    def _():
        xhr[...] = jnp.zeros(xhr.shape, jnp.bfloat16)

    p_taps, q_taps = stencil_zx()
    dzx[0:128] = p_taps.astype(jnp.bfloat16)
    dzx[128:256] = q_taps.astype(jnp.bfloat16)
    src = lax.broadcasted_iota(jnp.int32, (PAD, LC), 0)
    dst = lax.broadcasted_iota(jnp.int32, (PAD, LC), 1)
    for i in range(0, LC + 2 * PAD, PAD):
        dy[i : i + PAD] = (2.0 * taps(src - dst + (i - PAD))).astype(jnp.bfloat16)

    def z_copy(k, up, across):
        there = lax.rem(d + (1 if up else nd - 1), nd)
        lane = pl.multiple_of(chunk(k, there // per) * LC, LC)
        inner = pl.ds(pl.multiple_of(lane + PAD, PAD), LC)
        if across:
            src = v_ref.at[pl.ds(nz - 2 if up else 0, 2), :, pl.ds(lane, LC)]
        else:
            src = vp.at[pl.ds(nz if up else 2, 2), :, inner]
        return pltpu.make_async_remote_copy(
            src_ref=src,
            dst_ref=vp.at[pl.ds(0 if up else nz + 2, 2), :, inner],
            send_sem=zs.at[1 - up, k], recv_sem=zr.at[1 - up, k],
            device_id=(there, t), device_id_type=MESH,
        )

    def z_arrival(k, up):
        lane = pl.multiple_of(chunk(k) * LC, LC)
        return pltpu.make_async_remote_copy(
            src_ref=v_ref.at[pl.ds(0, 2), :, pl.ds(lane, LC)],
            dst_ref=vp.at[pl.ds(0 if up else nz + 2, 2), :, pl.ds(pl.multiple_of(lane + PAD, PAD), LC)],
            send_sem=zs.at[1 - up, k], recv_sem=zr.at[1 - up, k],
            device_id=(d, t), device_id_type=MESH,
        )

    def x_up(k):
        return pltpu.make_async_remote_copy(
            src_ref=ehi.at[k], dst_ref=xhl.at[k],
            send_sem=xs.at[0, k], recv_sem=xr.at[0, k],
            device_id=(d, lax.rem(t + 1, nt)), device_id_type=MESH,
        )

    def x_down(k):
        return pltpu.make_async_remote_copy(
            src_ref=elo.at[k], dst_ref=xhr.at[k],
            send_sem=xs.at[1, k], recv_sem=xr.at[1, k],
            device_id=(d, lax.rem(t + nt - 1, nt)), device_id_type=MESH,
        )

    for k in range(nc):
        load(k).wait()
        lane = pl.multiple_of(chunk(k) * LC, LC)
        rows = vp[2 : 2 + nz, :, pl.ds(pl.multiple_of(lane + PAD, PAD), LC)]
        elo[k] = rows[:, 0:2].reshape(nz * 2, LC)
        ehi[k] = rows[:, cx - 2 : cx].reshape(nz * 2, LC)
        if k == 0:
            waits = per - 1 + nc - 1
            for there in (t > 0, t < nt - 1, crosses_up, crosses_down):
                waits = waits + there.astype(jnp.int32)
            pl.semaphore_wait(barrier, waits)

        @pl.when(col < per - 1)
        def _():
            z_copy(k, True, False).start()

        @pl.when(col > 0)
        def _():
            z_copy(k, False, False).start()

        @pl.when(crosses_up)
        def _():
            z_copy(k, True, True).start()

        @pl.when(crosses_down)
        def _():
            z_copy(k, False, True).start()

        @pl.when(t < nt - 1)
        def _():
            x_up(k).start()

        @pl.when(t > 0)
        def _():
            x_down(k).start()

    for i in range(1, nc):
        pl.semaphore_signal(
            ready, inc=1, device_id=(lax.rem(row + i, nc) * per + col, t), device_id_type=MESH
        )

    def before_halo(k, _):
        lane = pl.multiple_of(chunk(k) * LC, LC)
        total = jnp.zeros((cx, LC), jnp.float32)
        last = jnp.ones((cx, LC), jnp.float32)
        sum1 = total
        sum2 = total
        part = min(256 // cx, nz)
        for z0 in range(0, nz, part):
            slab = vp[2 + z0 : 2 + z0 + part, :, pl.ds(lane, LC + 2 * PAD)]
            slab = slab.reshape(part * cx, LC + 2 * PAD)
            g = jnp.dot(slab, dy[...], preferred_element_type=jnp.float32)
            gy2[k, z0 * cx : (z0 + part) * cx] = g
            gyq[k, z0 * cx : (z0 + part) * cx] = g * g * 1.25 + 720.0
            for z in range(z0, z0 + part):
                f = vp[2 + z, :, pl.ds(pl.multiple_of(lane + PAD, PAD), LC)].astype(jnp.float32)
                ff = f * f
                total = total + ff
                now = jnp.exp2(total * -scale - scale * (z + 1))
                w = last - now
                wf = w * f
                wff = w * ff
                here = slice(z * cx, (z + 1) * cx)
                wt[k, here] = w
                wt1[k, here] = wf
                wt2[k, here] = wff
                sum1 = sum1 + wf
                sum2 = sum2 + wff
                last = now
        ss[k, 0] = BASE * (1.0 - last)
        ss[k, 1] = BASE * sum1
        ss[k, 2] = BASE * sum2
        ss[k, 3] = total * scale + scale * nz
        return 0

    lax.fori_loop(0, nc, before_halo, 0)
    pl.semaphore_wait(ready, nc - 1)

    low = lax.broadcasted_iota(jnp.int32, (cx, 128), 1) < OW

    def send(owner):
        return pltpu.make_async_remote_copy(
            src_ref=sb.at[owner], dst_ref=rb.at[d],
            send_sem=cs.at[owner], recv_sem=cr.at[d],
            device_id=(owner, t), device_id_type=MESH,
        )

    def arrival(i):
        return pltpu.make_async_remote_copy(
            src_ref=sb.at[i], dst_ref=rb.at[i],
            send_sem=cs.at[i], recv_sem=cr.at[i],
            device_id=(d, t), device_id_type=MESH,
        )

    def wait_halo(k):
        @pl.when(t > 0)
        def _():
            x_up(k).wait_recv()

        @pl.when(t < nt - 1)
        def _():
            x_down(k).wait_recv()

        @pl.when(d > 0)
        def _():
            z_arrival(k, True).wait_recv()

        @pl.when(d < nd - 1)
        def _():
            z_arrival(k, False).wait_recv()

    def stencil(k, z0):
        lane = pl.multiple_of(chunk(k) * LC, LC)
        slab = jnp.concatenate(
            [
                vp[z0 : z0 + ZB + 4, :, pl.ds(pl.multiple_of(lane + PAD, PAD), LC)].reshape((ZB + 4) * cx, LC),
                xhl[k, z0 * 2 : (z0 + ZB) * 2],
                xhr[k, z0 * 2 : (z0 + ZB) * 2],
                jnp.zeros((32, LC), jnp.bfloat16),
            ],
            axis=0,
        )
        return jnp.dot(dzx[...], slab, preferred_element_type=jnp.float32)

    def after_halo(k, _):
        m0, m1, m2 = ss[k, 0], ss[k, 1], ss[k, 2]
        wait_halo(k)
        for z0 in range(0, nz, ZB):
            g = stencil(k, z0)
            for j in range(ZB):
                here = slice((z0 + j) * cx, (z0 + j + 1) * cx)
                p = g[j * cx : (j + 1) * cx]
                q = g[128 + j * cx : 128 + (j + 1) * cx]
                facing = jnp.abs(p + gy2[k, here])
                facing = facing * lax.rsqrt(p * p + q * q + gyq[k, here])
                m0 = m0 + facing * wt[k, here]
                m1 = m1 + facing * wt1[k, here]
                m2 = m2 + facing * wt2[k, here]
        s = ss[k, 3]
        for q in range(per):
            part = slice((q // 2) * 128, (q // 2 + 1) * 128)
            a, b, c, e = m0[:, part], m1[:, part], m2[:, part], s[:, part]
            if q % 2 == 0:
                first = jnp.where(low, a, pltpu.roll(b, OW, 1))
                second = jnp.where(low, c, pltpu.roll(e, OW, 1))
            else:
                first = jnp.where(low, pltpu.roll(a, OW, 1), b)
                second = jnp.where(low, pltpu.roll(c, OW, 1), e)
            owner = chunk(k) * per + q

            @pl.when(owner != d)
            def _():
                sb[owner, 0] = encode(first)
                sb[owner, 1] = encode(second)
                send(owner).start()

            @pl.when(owner == d)
            def _():
                got[d, 0] = first
                got[d, 1] = second

        return 0

    lax.fori_loop(0, nc, after_halo, 0)

    def take(r, q):
        @pl.when((r != row) | (q != col))
        def _():
            i = r * per + q
            arrival(i).wait_recv()
            got[i] = decode(rb[i])

    def other_row(n, _):
        for q in range(per):
            take(lax.rem(row + n, nc), q)
        return 0

    lax.fori_loop(1, nc, other_row, 0)
    for k in range(nc):

        @pl.when(t < nt - 1)
        def _():
            x_up(k).wait_send()

        @pl.when(t > 0)
        def _():
            x_down(k).wait_send()

        @pl.when(d < nd - 1)
        def _():
            z_copy(k, True, False).wait_send()

        @pl.when(d > 0)
        def _():
            z_copy(k, False, False).wait_send()

    for i in range(nd):

        @pl.when(d != i)
        def _():
            send(i).wait_send()
    for q in range(per):
        take(row, q)
    ahead = jnp.zeros((cx, 128), jnp.float32)
    acc0 = ahead
    acc1 = ahead
    for i in range(nd):
        p0, p1 = got[i, 0], got[i, 1]
        through = jnp.exp2(-ahead)
        acc0 = acc0 + through * p0
        acc1 = acc1 + through * p1
        ahead = ahead + jnp.where(low, pltpu.roll(p1, OW, 1), p1)
    a = acc0 * GAIN
    b = pltpu.roll(a, OW, 1)
    c = acc1 * GAIN
    o_ref[0] = (a + 0.5 * b)[:, :OW]
    o_ref[1] = (a - 0.3 * b + 0.2 * c)[:, :OW]
    o_ref[2] = (a + 0.25 * b - 0.1 * c)[:, :OW]
    o_ref[3] = (1.0 - jnp.exp2(-ahead))[:, :OW]


def solution(mesh):
    nd, nt = mesh.shape["depth"], mesh.shape["tile"]

    def body(volume):
        nz, cx, ny = volume.shape
        nc = ny // LC
        big = (nc, nz * cx, LC)
        return pl.pallas_call(
            functools.partial(kernel, nd, nt),
            out_shape=jax.ShapeDtypeStruct((4, cx, OW), jnp.float32),
            in_specs=[pl.BlockSpec(memory_space=pl.ANY)],
            out_specs=pl.BlockSpec(memory_space=pltpu.VMEM),
            scratch_shapes=[
                pltpu.VMEM((nz + 4, cx, ny + 2 * PAD), jnp.bfloat16),
                pltpu.VMEM((nc, nz * 2, LC), jnp.bfloat16),
                pltpu.VMEM((nc, nz * 2, LC), jnp.bfloat16),
                pltpu.VMEM((nc, nz * 2, LC), jnp.bfloat16),
                pltpu.VMEM((nc, nz * 2, LC), jnp.bfloat16),
                pltpu.VMEM(big, jnp.float32),
                pltpu.VMEM(big, jnp.float32),
                pltpu.VMEM(big, jnp.float32),
                pltpu.VMEM(big, jnp.float32),
                pltpu.VMEM(big, jnp.float32),
                pltpu.VMEM((nc, 4, cx, LC), jnp.float32),
                pltpu.VMEM((256, 256), jnp.bfloat16),
                pltpu.VMEM((LC + 2 * PAD, LC), jnp.bfloat16),
                pltpu.VMEM((nd, 2, cx, 128), jnp.bfloat16),
                pltpu.VMEM((nd, 2, cx, 128), jnp.bfloat16),
                pltpu.VMEM((nd, 2, cx, 128), jnp.float32),
                pltpu.SemaphoreType.DMA((nc,)),
                pltpu.SemaphoreType.DMA((2, nc)),
                pltpu.SemaphoreType.DMA((2, nc)),
                pltpu.SemaphoreType.DMA((2, nc)),
                pltpu.SemaphoreType.DMA((2, nc)),
                pltpu.SemaphoreType.DMA((nd,)),
                pltpu.SemaphoreType.DMA((nd,)),
                pltpu.SemaphoreType.REGULAR,
            ],
            compiler_params=pltpu.CompilerParams(
                collective_id=0, has_side_effects=True, vmem_limit_bytes=105 * 2**19
            ),
        )(volume)

    return jax.shard_map(
        body,
        mesh=mesh,
        in_specs=(P("depth", "tile", None),),
        out_specs=P(None, "tile", "depth"),
        check_vma=False,
    )
```

```python
import functools
import math

import jax
import jax.numpy as jnp
from jax import lax
from jax.experimental import pallas as pl
from jax.experimental.pallas import tpu as pltpu
from jax.sharding import PartitionSpec as P

MESH = pl.DeviceIdType.MESH
LC = 256
OW = 64
ZB = 8
PAD = 128
BASE = 0.15 * 3.0 / 0.85 / math.sqrt(5.0)
CODE = 44.0
GAIN = 0.85 / 3.0 * math.sqrt(5.0)


def taps(delta):
    value = jnp.where(delta == -2, 1.0, 0.0)
    value = jnp.where(delta == -1, -8.0, value)
    value = jnp.where(delta == 1, 8.0, value)
    return jnp.where(delta == 2, -1.0, value)


def stencil_zx():
    out = lax.broadcasted_iota(jnp.int32, (128, 256), 0)
    col = lax.broadcasted_iota(jnp.int32, (128, 256), 1)
    zo, xo = out >> 4, out & 15
    zi, xi = (col >> 4) - 2, col & 15
    inside = col < 192
    gz = jnp.where(inside & (xi == xo), taps(zi - zo), 0.0)
    k = col & 15
    pos = (k & 1) + jnp.where(col >= 208, 16, -2)
    plane = jnp.where(inside, zi, jnp.where(col < 224, k >> 1, -9))
    gx = jnp.where(plane == zo, taps(jnp.where(inside, xi, pos) - xo), 0.0)
    return gx + 2.0 * gz, 2.0 * gx - gz


def encode(value):
    v = value * CODE
    v2 = v * v
    v4 = v2 * v2
    return (v4 * v4 * v2 * v).astype(jnp.bfloat16)


def decode(code):
    u = code.astype(jnp.float32)
    size = jnp.exp2(jnp.log2(jnp.maximum(jnp.abs(u), 1e-37)) * (1.0 / 11.0) - math.log2(CODE))
    return jnp.where(u < 0.0, -size, size)


def kernel(nd, nt, v_ref, o_ref, vp, xhl, xhr, elo, ehi, gy2, gyq, wt, wt1, wt2, ss, dzx, dy,
           sb, rb, got, load_sem, zs, zr, xs, xr, cs, cr, ready):
    nz, cx, ny = v_ref.shape
    nc = ny // LC
    per = LC // OW
    d = lax.axis_index("depth")
    t = lax.axis_index("tile")
    row, col = d // per, lax.rem(d, per)
    scale = math.log2(math.e) / (nz * nd)

    barrier = pltpu.get_barrier_semaphore()

    def greet(depth, tile):
        pl.semaphore_signal(barrier, inc=1, device_id=(depth, tile), device_id_type=MESH)

    for i in range(1, per):
        greet(row * per + lax.rem(col + i, per), t)

    @pl.when(t > 0)
    def _():
        greet(d, t - 1)

    @pl.when(t < nt - 1)
    def _():
        greet(d, t + 1)

    crosses_up = (col == per - 1) & (d < nd - 1)
    crosses_down = (col == 0) & (d > 0)

    @pl.when(crosses_up)
    def _():
        greet(d + 1, t)

    @pl.when(crosses_down)
    def _():
        greet(d - 1, t)

    def chunk(k, r=None):
        r = row if r is None else r
        if nc != 4:
            return lax.rem(r + 1 + k, nc)
        if isinstance(k, int):
            return lax.rem(r + (2, 1, 3, 0)[k], nc)
        return lax.rem(r + jnp.where(k == 3, 0, jnp.where(k == 2, 3, 2 - k)), nc)

    def load(k):
        lane = pl.multiple_of(chunk(k) * LC, LC)
        return pltpu.make_async_copy(
            v_ref.at[:, :, pl.ds(lane, LC)],
            vp.at[pl.ds(2, nz), :, pl.ds(pl.multiple_of(lane + PAD, PAD), LC)],
            load_sem.at[k],
        )

    for k in range(nc):
        load(k).start()

    for i in range(1, nc):
        greet(lax.rem(row + i, nc) * per + col, t)

    zeros = jnp.zeros((nz, cx, PAD), jnp.bfloat16)
    vp[2 : 2 + nz, :, 0:PAD] = zeros
    vp[2 : 2 + nz, :, PAD + ny :] = zeros

    @pl.when(d == 0)
    def _():
        vp[0:2] = jnp.zeros((2, cx, ny + 2 * PAD), jnp.bfloat16)

    @pl.when(d == nd - 1)
    def _():
        vp[nz + 2 :] = jnp.zeros((2, cx, ny + 2 * PAD), jnp.bfloat16)

    @pl.when(t == 0)
    def _():
        xhl[...] = jnp.zeros(xhl.shape, jnp.bfloat16)

    @pl.when(t == nt - 1)
    def _():
        xhr[...] = jnp.zeros(xhr.shape, jnp.bfloat16)

    p_taps, q_taps = stencil_zx()
    dzx[0:128] = p_taps.astype(jnp.bfloat16)
    dzx[128:256] = q_taps.astype(jnp.bfloat16)
    src = lax.broadcasted_iota(jnp.int32, (PAD, LC), 0)
    dst = lax.broadcasted_iota(jnp.int32, (PAD, LC), 1)
    for i in range(0, LC + 2 * PAD, PAD):
        dy[i : i + PAD] = (2.0 * taps(src - dst + (i - PAD))).astype(jnp.bfloat16)

    def z_copy(k, up):
        there = lax.rem(d + (1 if up else nd - 1), nd)
        lane = pl.multiple_of(chunk(k, there // per) * LC, LC)
        inner = pl.ds(pl.multiple_of(lane + PAD, PAD), LC)
        src = vp.at[pl.ds(nz if up else 2, 2), :, inner]
        return pltpu.make_async_remote_copy(
            src_ref=src,
            dst_ref=vp.at[pl.ds(0 if up else nz + 2, 2), :, inner],
            send_sem=zs.at[1 - up, k], recv_sem=zr.at[1 - up, k],
            device_id=(there, t), device_id_type=MESH,
        )

    def z_arrival(k, up):
        lane = pl.multiple_of(chunk(k) * LC, LC)
        return pltpu.make_async_remote_copy(
            src_ref=v_ref.at[pl.ds(0, 2), :, pl.ds(lane, LC)],
            dst_ref=vp.at[pl.ds(0 if up else nz + 2, 2), :, pl.ds(pl.multiple_of(lane + PAD, PAD), LC)],
            send_sem=zs.at[1 - up, k], recv_sem=zr.at[1 - up, k],
            device_id=(d, t), device_id_type=MESH,
        )

    def x_up(k):
        return pltpu.make_async_remote_copy(
            src_ref=ehi.at[k], dst_ref=xhl.at[k],
            send_sem=xs.at[0, k], recv_sem=xr.at[0, k],
            device_id=(d, lax.rem(t + 1, nt)), device_id_type=MESH,
        )

    def x_down(k):
        return pltpu.make_async_remote_copy(
            src_ref=elo.at[k], dst_ref=xhr.at[k],
            send_sem=xs.at[1, k], recv_sem=xr.at[1, k],
            device_id=(d, lax.rem(t + nt - 1, nt)), device_id_type=MESH,
        )

    crosses = crosses_up | crosses_down
    for k in range(nc):
        if k == 0:
            load(0).wait()

            @pl.when(crosses)
            def _():
                for later in range(1, nc):
                    load(later).wait()

        else:

            @pl.when(jnp.logical_not(crosses))
            def _():
                load(k).wait()

        lane = pl.multiple_of(chunk(k) * LC, LC)
        rows = vp[2 : 2 + nz, :, pl.ds(pl.multiple_of(lane + PAD, PAD), LC)]
        elo[k] = rows[:, 0:2].reshape(nz * 2, LC)
        ehi[k] = rows[:, cx - 2 : cx].reshape(nz * 2, LC)
        if k == 0:
            waits = per - 1 + nc - 1
            for there in (t > 0, t < nt - 1, crosses_up, crosses_down):
                waits = waits + there.astype(jnp.int32)
            pl.semaphore_wait(barrier, waits)

        @pl.when(d < nd - 1)
        def _():
            z_copy(k, True).start()

        @pl.when(d > 0)
        def _():
            z_copy(k, False).start()

        @pl.when(t < nt - 1)
        def _():
            x_up(k).start()

        @pl.when(t > 0)
        def _():
            x_down(k).start()

    for i in range(1, nc):
        pl.semaphore_signal(
            ready, inc=1, device_id=(lax.rem(row + i, nc) * per + col, t), device_id_type=MESH
        )

    def before_halo(k, _):
        lane = pl.multiple_of(chunk(k) * LC, LC)
        total = jnp.zeros((cx, LC), jnp.float32)
        last = jnp.ones((cx, LC), jnp.float32)
        sum1 = total
        sum2 = total
        part = min(256 // cx, nz)
        for z0 in range(0, nz, part):
            slab = vp[2 + z0 : 2 + z0 + part, :, pl.ds(lane, LC + 2 * PAD)]
            slab = slab.reshape(part * cx, LC + 2 * PAD)
            g = jnp.dot(slab, dy[...], preferred_element_type=jnp.float32)
            gy2[k, z0 * cx : (z0 + part) * cx] = g
            gyq[k, z0 * cx : (z0 + part) * cx] = g * g * 1.25 + 720.0
            for z in range(z0, z0 + part):
                f = vp[2 + z, :, pl.ds(pl.multiple_of(lane + PAD, PAD), LC)].astype(jnp.float32)
                ff = f * f
                total = total + ff
                now = jnp.exp2(total * -scale - scale * (z + 1))
                w = last - now
                wf = w * f
                wff = w * ff
                here = slice(z * cx, (z + 1) * cx)
                wt[k, here] = w
                wt1[k, here] = wf
                wt2[k, here] = wff
                sum1 = sum1 + wf
                sum2 = sum2 + wff
                last = now
        ss[k, 0] = BASE * (1.0 - last)
        ss[k, 1] = BASE * sum1
        ss[k, 2] = BASE * sum2
        ss[k, 3] = total * scale + scale * nz
        return 0

    lax.fori_loop(0, nc, before_halo, 0)
    pl.semaphore_wait(ready, nc - 1)

    low = lax.broadcasted_iota(jnp.int32, (cx, 128), 1) < OW

    def send(owner):
        return pltpu.make_async_remote_copy(
            src_ref=sb.at[owner], dst_ref=rb.at[d],
            send_sem=cs.at[owner], recv_sem=cr.at[d],
            device_id=(owner, t), device_id_type=MESH,
        )

    def arrival(i):
        return pltpu.make_async_remote_copy(
            src_ref=sb.at[i], dst_ref=rb.at[i],
            send_sem=cs.at[i], recv_sem=cr.at[i],
            device_id=(d, t), device_id_type=MESH,
        )

    def wait_halo(k):
        @pl.when(t > 0)
        def _():
            x_up(k).wait_recv()

        @pl.when(t < nt - 1)
        def _():
            x_down(k).wait_recv()

        @pl.when(d > 0)
        def _():
            z_arrival(k, True).wait_recv()

        @pl.when(d < nd - 1)
        def _():
            z_arrival(k, False).wait_recv()

    def stencil(k, z0):
        lane = pl.multiple_of(chunk(k) * LC, LC)
        slab = jnp.concatenate(
            [
                vp[z0 : z0 + ZB + 4, :, pl.ds(pl.multiple_of(lane + PAD, PAD), LC)].reshape((ZB + 4) * cx, LC),
                xhl[k, z0 * 2 : (z0 + ZB) * 2],
                xhr[k, z0 * 2 : (z0 + ZB) * 2],
                jnp.zeros((32, LC), jnp.bfloat16),
            ],
            axis=0,
        )
        return jnp.dot(dzx[...], slab, preferred_element_type=jnp.float32)

    def after_halo(k, _):
        m0, m1, m2 = ss[k, 0], ss[k, 1], ss[k, 2]
        wait_halo(k)
        for z0 in range(0, nz, ZB):
            g = stencil(k, z0)
            for j in range(ZB):
                here = slice((z0 + j) * cx, (z0 + j + 1) * cx)
                p = g[j * cx : (j + 1) * cx]
                q = g[128 + j * cx : 128 + (j + 1) * cx]
                facing = jnp.abs(p + gy2[k, here])
                facing = facing * lax.rsqrt(p * p + q * q + gyq[k, here])
                m0 = m0 + facing * wt[k, here]
                m1 = m1 + facing * wt1[k, here]
                m2 = m2 + facing * wt2[k, here]
        s = ss[k, 3]
        for q in range(per):
            part = slice((q // 2) * 128, (q // 2 + 1) * 128)
            a, b, c, e = m0[:, part], m1[:, part], m2[:, part], s[:, part]
            if q % 2 == 0:
                first = jnp.where(low, a, pltpu.roll(b, OW, 1))
                second = jnp.where(low, c, pltpu.roll(e, OW, 1))
            else:
                first = jnp.where(low, pltpu.roll(a, OW, 1), b)
                second = jnp.where(low, pltpu.roll(c, OW, 1), e)
            owner = chunk(k) * per + q

            @pl.when(owner != d)
            def _():
                sb[owner, 0] = encode(first)
                sb[owner, 1] = encode(second)
                send(owner).start()

            @pl.when(owner == d)
            def _():
                got[d, 0] = first
                got[d, 1] = second

        return 0

    lax.fori_loop(0, nc, after_halo, 0)

    def take(r, q):
        @pl.when((r != row) | (q != col))
        def _():
            i = r * per + q
            arrival(i).wait_recv()
            got[i] = decode(rb[i])

    def other_row(n, _):
        for q in range(per):
            take(lax.rem(row + n, nc), q)
        return 0

    lax.fori_loop(1, nc, other_row, 0)
    for k in range(nc):

        @pl.when(t < nt - 1)
        def _():
            x_up(k).wait_send()

        @pl.when(t > 0)
        def _():
            x_down(k).wait_send()

        @pl.when(d < nd - 1)
        def _():
            z_copy(k, True).wait_send()

        @pl.when(d > 0)
        def _():
            z_copy(k, False).wait_send()

    for i in range(nd):

        @pl.when(d != i)
        def _():
            send(i).wait_send()
    for q in range(per):
        take(row, q)
    ahead = jnp.zeros((cx, 128), jnp.float32)
    acc0 = ahead
    acc1 = ahead
    for i in range(nd):
        p0, p1 = got[i, 0], got[i, 1]
        through = jnp.exp2(-ahead)
        acc0 = acc0 + through * p0
        acc1 = acc1 + through * p1
        ahead = ahead + jnp.where(low, pltpu.roll(p1, OW, 1), p1)
    a = acc0 * GAIN
    b = pltpu.roll(a, OW, 1)
    c = acc1 * GAIN
    o_ref[0] = (a + 0.5 * b)[:, :OW]
    o_ref[1] = (a - 0.3 * b + 0.2 * c)[:, :OW]
    o_ref[2] = (a + 0.25 * b - 0.1 * c)[:, :OW]
    o_ref[3] = (1.0 - jnp.exp2(-ahead))[:, :OW]


def solution(mesh):
    nd, nt = mesh.shape["depth"], mesh.shape["tile"]

    def body(volume):
        nz, cx, ny = volume.shape
        nc = ny // LC
        big = (nc, nz * cx, LC)
        return pl.pallas_call(
            functools.partial(kernel, nd, nt),
            out_shape=jax.ShapeDtypeStruct((4, cx, OW), jnp.float32),
            in_specs=[pl.BlockSpec(memory_space=pl.ANY)],
            out_specs=pl.BlockSpec(memory_space=pltpu.VMEM),
            scratch_shapes=[
                pltpu.VMEM((nz + 4, cx, ny + 2 * PAD), jnp.bfloat16),
                pltpu.VMEM((nc, nz * 2, LC), jnp.bfloat16),
                pltpu.VMEM((nc, nz * 2, LC), jnp.bfloat16),
                pltpu.VMEM((nc, nz * 2, LC), jnp.bfloat16),
                pltpu.VMEM((nc, nz * 2, LC), jnp.bfloat16),
                pltpu.VMEM(big, jnp.float32),
                pltpu.VMEM(big, jnp.float32),
                pltpu.VMEM(big, jnp.float32),
                pltpu.VMEM(big, jnp.float32),
                pltpu.VMEM(big, jnp.float32),
                pltpu.VMEM((nc, 4, cx, LC), jnp.float32),
                pltpu.VMEM((256, 256), jnp.bfloat16),
                pltpu.VMEM((LC + 2 * PAD, LC), jnp.bfloat16),
                pltpu.VMEM((nd, 2, cx, 128), jnp.bfloat16),
                pltpu.VMEM((nd, 2, cx, 128), jnp.bfloat16),
                pltpu.VMEM((nd, 2, cx, 128), jnp.float32),
                pltpu.SemaphoreType.DMA((nc,)),
                pltpu.SemaphoreType.DMA((2, nc)),
                pltpu.SemaphoreType.DMA((2, nc)),
                pltpu.SemaphoreType.DMA((2, nc)),
                pltpu.SemaphoreType.DMA((2, nc)),
                pltpu.SemaphoreType.DMA((nd,)),
                pltpu.SemaphoreType.DMA((nd,)),
                pltpu.SemaphoreType.REGULAR,
            ],
            compiler_params=pltpu.CompilerParams(
                collective_id=0, has_side_effects=True, vmem_limit_bytes=105 * 2**19
            ),
        )(volume)

    return jax.shard_map(
        body,
        mesh=mesh,
        in_specs=(P("depth", "tile", None),),
        out_specs=P(None, "tile", "depth"),
        check_vma=False,
    )
```
